256 devices in a mesh: ctx: 64 (over x, z, core), head: 4 (over y).
Axes of the slice: x: 4, y: 4, z: 8, core: 2. Of those that a mesh axis runs over, the one named last changes fastest.
Arguments:
- queries: bfloat16 [8192, 64, 576], P('ctx', 'head'), may hold values from -32 to 32
- latent: bfloat16 [8192, 576], P('ctx'), may hold values from -4 to 4
- grad_out: bfloat16 [8192, 64, 512], P('ctx', 'head'), may hold values from -0.29882812 to 0.29882812
- doc_start: int32 [8192], P('ctx'), may hold values from 0 to 8191, as said below
- block_list: int32 [64, 4], P('ctx'), may hold values from -1 to 63, as said below
Outputs:
- attended: bfloat16 [8192, 64, 512], P('ctx', 'head')
- grad_queries: float32 [8192, 64, 576], P('ctx', 'head')
- grad_latent: float32 [8192, 576], P('ctx', 'head')
The draws below stay inside these ranges and needn't reach their ends.
Inputs may be any that keep to these rules, and one draw needn't show every extreme that they name: Documents are contiguous runs of tokens, each of at most 384 tokens and one of exactly 384; the last token of the sequence is a document of its own; doc_start[i] is the first position of token i's run. `block_list`: row b lists, ascending, every block from the one that holds doc_start[b * 128] through b, then -1; so it holds at most 4 blocks, always b, and some row holds exactly 4.
All inputs are finite; a program needn't handle non-finite values.
Results may differ from the reference program's by a relative error of at most 0.014.
Values may be sent and summed in bfloat16 or wider, within the bound.
No kernel may reach another device: no remote copies, remote signals or barrier semaphores. Data moves between devices by JAX's collectives and lax.ppermute only.
A program may use at most 128 MiB of HBM per device.

```python
import math
import jax
import jax.numpy as jnp
from jax import lax

LAT = 512
ROPE = 64
BLK = 128
NB = 4
SEQ = 8192
NQB = 64
HEADS = 64
MAXDOC = 384


def latent_base(key):
    normal_part = jax.random.normal(key, (SEQ, LAT + ROPE), jnp.float32)
    return jnp.clip(normal_part, -4.0, 4.0)


def document_tables(key):
    key_short, key_long, key_first = jax.random.split(key, 3)
    short_len = jax.random.randint(key_short, (SEQ,), 1, min(2 * BLK, MAXDOC) + 1)
    long_flag = jax.random.randint(key_long, (SEQ,), 0, 3) == 0
    lengths = jnp.where(long_flag, MAXDOC, short_len).astype(jnp.int32)
    first_len = jax.random.randint(key_first, (), 1, BLK)
    lengths = lengths.at[0].set(first_len).at[1].set(MAXDOC)
    ends = jnp.cumsum(lengths).astype(jnp.int32)
    starts = jnp.concatenate([jnp.zeros((1,), jnp.int32), ends[:-1]])
    positions = jnp.arange(SEQ, dtype=jnp.int32)
    doc_index = jnp.searchsorted(ends, positions, side='right').astype(jnp.int32)
    doc_first = jnp.take(starts, doc_index).astype(jnp.int32)
    doc_first = jnp.where(positions == SEQ - 1, SEQ - 1, doc_first).astype(jnp.int32)
    block_ids = jnp.arange(NQB, dtype=jnp.int32)
    first_block = jnp.take(doc_first, block_ids * BLK) // BLK
    entries = first_block[:, None] + jnp.arange(NB, dtype=jnp.int32)[None, :]
    lists = jnp.where(entries <= block_ids[:, None], entries, -1).astype(jnp.int32)
    return (doc_first, lists)


def draw_latent(key, part):
    return latent_base(key).astype(jnp.bfloat16)


def draw_queries(key, part):
    key = jax.random.fold_in(key, 1)
    values = jnp.clip(jax.random.normal(key, (SEQ, HEADS, LAT + ROPE), jnp.float32), -4.0, 4.0)
    return values.astype(jnp.bfloat16)


def draw_doc_start(key, part):
    doc_first, lists = document_tables(key)
    return doc_first


def draw_block_list(key, part):
    doc_first, lists = document_tables(key)
    return lists


def block_levels(key, dims, pieces, low, largest):
    factor_of = 1.0
    for position, shards_of in pieces:
        draws = jax.random.uniform(jax.random.fold_in(jax.random.fold_in(key, 6), position), (shards_of,), jnp.float32, low / len(pieces), largest / len(pieces))
        factor_of = factor_of * jnp.repeat(jnp.exp(draws), dims[position] // shards_of).reshape((-1,) + (1,) * (len(dims) - 1 - position))
    return factor_of


def noise(stream_key, dims, deviation, most, shards=(), held_as=jnp.bfloat16):
    drawn = deviation * jax.random.normal(stream_key, dims, jnp.float32)
    if shards:
        drawn = drawn * block_levels(stream_key, dims, shards, -0.22, 0.18)
    return jnp.clip(drawn, -most, most).astype(held_as)


def setup_inputs(seed: int = 0) -> dict:
    arg_keys = jax.random.split(jax.random.key(seed), 6)
    return {
        "queries": draw_queries(jax.random.fold_in(arg_keys[5], 71), 0),
        "latent": draw_latent(jax.random.fold_in(arg_keys[5], 71), 0),
        "grad_out": noise(arg_keys[2], (SEQ, HEADS, LAT), 0.05, 0.29882812, ((0, 64), (1, 4))),
        "doc_start": draw_doc_start(jax.random.fold_in(arg_keys[5], 71), 0),
        "block_list": draw_block_list(jax.random.fold_in(arg_keys[5], 71), 0),
    }


def wide(value):
    return value.astype(jnp.float32)

def block_terms(q_rows, grad_rows, q_pos, q_start, entries, latent, score_scale, grad_latent):
    block_rows = q_rows.shape[0]
    heads = q_rows.shape[1]
    latent_width = grad_rows.shape[2]
    full_width = latent.shape[1]
    listed = jnp.sum((entries >= 0).astype(jnp.int32))

    def score_block(slot):
        entry = entries[slot]
        row_start = (entry * block_rows).astype(jnp.int32)
        key_rows = lax.dynamic_slice_in_dim(latent, row_start, block_rows, 0)
        key_pos = row_start + jnp.arange(block_rows, dtype=jnp.int32)
        allowed = (key_pos[None, :] <= q_pos[:, None]) & (key_pos[None, :] >= q_start[:, None])
        score = jnp.einsum('qhc,kc->hqk', wide(q_rows), wide(key_rows)) * score_scale
        return (key_rows, score, allowed[None, :, :], row_start)

    def stat_step(slot, carry):
        run_max, run_sum = carry
        key_rows, score, allowed, row_start = score_block(slot)
        block_top = lax.optimization_barrier(jnp.max(jnp.where(allowed, score, -1e+30), axis=2))
        new_max = jnp.maximum(run_max, block_top)
        terms = jnp.where(allowed, jnp.exp(score - new_max[:, :, None]), 0.0)
        return (new_max, run_sum * jnp.exp(run_max - new_max) + lax.optimization_barrier(jnp.sum(terms, axis=2)))
    start_max = jnp.full((heads, block_rows), -1e+30, jnp.float32)
    start_sum = jnp.zeros((heads, block_rows), jnp.float32)
    run_max, run_sum = lax.fori_loop(0, listed, stat_step, (start_max, start_sum))
    lse = run_max + jnp.log(run_sum)

    def weights_of(slot):
        key_rows, score, allowed, row_start = score_block(slot)
        weight = jnp.where(allowed, jnp.exp(score - lse[:, :, None]), 0.0)
        weight_b = lax.optimization_barrier(weight.astype(jnp.bfloat16))
        return (key_rows, weight, weight_b, row_start)

    def out_step(slot, total):
        key_rows, weight, weight_b, row_start = weights_of(slot)
        return total + jnp.einsum('hqk,kl->qhl', wide(weight_b), wide(key_rows[:, :latent_width]))
    attended32 = lax.fori_loop(0, listed, out_step, jnp.zeros((block_rows, heads, latent_width), jnp.float32))
    attended = lax.optimization_barrier(attended32.astype(jnp.bfloat16))
    delta = jnp.einsum('qhl,qhl->hq', wide(grad_rows), wide(attended))

    def back_step(slot, carry):
        grad_query, grad_latent = carry
        key_rows, weight, weight_b, row_start = weights_of(slot)
        grad_weight = jnp.einsum('qhl,kl->hqk', wide(grad_rows), wide(key_rows[:, :latent_width]))
        grad_score = weight * (grad_weight - delta[:, :, None])
        grad_score_b = lax.optimization_barrier(grad_score.astype(jnp.bfloat16))
        grad_query = grad_query + score_scale * jnp.einsum('hqk,kc->qhc', wide(grad_score_b), wide(key_rows))
        grad_key = score_scale * jnp.einsum('hqk,qhc->kc', wide(grad_score_b), wide(q_rows))
        grad_value = jnp.einsum('hqk,qhl->kl', wide(weight_b), wide(grad_rows))
        grad_key = grad_key + jnp.pad(grad_value, ((0, 0), (0, full_width - latent_width)))
        current = lax.dynamic_slice_in_dim(grad_latent, row_start, block_rows, 0)
        grad_latent = lax.dynamic_update_slice_in_dim(grad_latent, current + grad_key, row_start, 0)
        return (grad_query, grad_latent)
    start_query = jnp.zeros((block_rows, heads, full_width), jnp.float32)
    grad_query, grad_latent = lax.fori_loop(0, listed, back_step, (start_query, grad_latent))
    return (attended, grad_query, grad_latent)

def reference(queries, latent, grad_out, doc_start, block_list):
    score_scale = 1.0 / math.sqrt(LAT // 4 + ROPE)

    def scan_step(grad_latent, block_index):
        row_start = (block_index * BLK).astype(jnp.int32)
        q_rows = lax.dynamic_slice_in_dim(queries, row_start, BLK, 0)
        grad_rows = lax.dynamic_slice_in_dim(grad_out, row_start, BLK, 0)
        q_start = lax.dynamic_slice_in_dim(doc_start, row_start, BLK, 0)
        q_pos = row_start + jnp.arange(BLK, dtype=jnp.int32)
        entries = block_list[block_index]
        attended, grad_query, grad_latent = block_terms(q_rows, grad_rows, q_pos, q_start, entries, latent, score_scale, grad_latent)
        return (grad_latent, (attended, grad_query))
    start = jnp.zeros((SEQ, LAT + ROPE), jnp.float32)
    grad_latent, stacked = lax.scan(scan_step, start, jnp.arange(NQB, dtype=jnp.int32))
    attended = stacked[0].reshape(SEQ, HEADS, LAT)
    grad_queries = stacked[1].reshape(SEQ, HEADS, LAT + ROPE)
    return (attended, grad_queries, grad_latent)
```

```python
import functools
import math

import jax
import jax.numpy as jnp
from jax import lax
from jax.experimental import pallas as pl
from jax.experimental.pallas import tpu as pltpu
from jax.sharding import PartitionSpec as P

F32 = jnp.float32
BF16 = jnp.bfloat16
GROUP = 4
NN = (((1,), (0,)), ((), ()))
NT = (((1,), (1,)), ((), ()))


def shifted(value, axis, steps):
    count = lax.axis_size(axis)
    return lax.ppermute(value, axis, [(s, (s + steps) % count) for s in range(count)])


def dot(a, b, dims=NN):
    return lax.dot_general(a, b, dims, preferred_element_type=F32)


def lanes(ref, count):
    return jnp.concatenate([ref[n] for n in range(count)], axis=1)


def backward_kernel(
    scale, place_ref, entries_ref, start_ref, *refs
):
    list_width = entries_ref.shape[1]
    key_refs = refs[:list_width]
    q_ref, g_ref, weight_ref, score_ref, out_ref, rows_ref, bias_ref, acc_ref = refs[list_width:]
    step = pl.program_id(0)
    width, block = key_refs[0].shape
    latent_width = g_ref.shape[1]
    keys = list_width * block
    place = place_ref[0]

    @pl.when(step == 0)
    def _():
        q_pos = place * block + lax.broadcasted_iota(jnp.int32, (block, block), 1)
        q_start = start_ref[...]
        for slot in range(list_width):
            rows_ref[slot * block : (slot + 1) * block, :] = key_refs[slot][...].T
            entry = place - (list_width - 1) + slot
            listed = entry < 0
            for n in range(list_width):
                listed = listed | (entries_ref[0, n] == entry)
            listed = listed & (entry >= 0)
            first = jnp.where(listed, entry * block, 1 << 24)
            k_pos = first + lax.broadcasted_iota(jnp.int32, (block, block), 0)
            allowed = (k_pos <= q_pos) & (k_pos >= q_start)
            bias_ref[slot * block : (slot + 1) * block, :] = jnp.where(allowed, 0.0, -1e30)
        acc_ref[...] = jnp.zeros_like(acc_ref)

    q_cols = lanes(q_ref, GROUP)
    g_cols = lanes(g_ref, GROUP)
    score = dot(rows_ref[...], q_cols)
    grad_weight = dot(rows_ref[:, :latent_width], g_cols)
    bias = jnp.concatenate([bias_ref[...]] * GROUP, axis=1)
    score = score * (scale * math.log2(math.e)) + bias
    top = jnp.max(score, axis=0, keepdims=True)
    terms = jnp.exp2(score - top)
    weight = terms * (1.0 / jnp.sum(terms, axis=0, keepdims=True))
    delta = jnp.sum(weight * grad_weight, axis=0, keepdims=True)
    grad_score = ((weight * scale) * (grad_weight - delta)).astype(BF16)
    weight_b = weight.astype(BF16)
    weight_ref[0] = weight_b
    score_ref[0] = grad_score
    acc_ref[...] += dot(q_cols, grad_score, NT)
    acc_ref[:latent_width, :] += dot(g_cols, weight_b, NT)

    @pl.when(step == pl.num_programs(0) - 1)
    def _():
        out_ref[...] = acc_ref[...].astype(BF16)


def forward_kernel(*refs):
    key_refs = refs[:-6]
    weight_ref, score_ref, att_ref, gq_ref, cols_ref, rows_ref = refs[-6:]
    block = key_refs[0].shape[1]
    latent_width = att_ref.shape[2]

    @pl.when(pl.program_id(0) == 0)
    def _():
        for slot, key_ref in enumerate(key_refs):
            cols_ref[:, slot * block : (slot + 1) * block] = key_ref[...]
            rows_ref[slot * block : (slot + 1) * block, :] = key_ref[:latent_width, :].T

    grad = dot(cols_ref[...], score_ref[0])
    for n in range(GROUP):
        gq_ref[n] = grad[:, n * block : (n + 1) * block]
    att = dot(weight_ref[0].T, rows_ref[...])
    for n in range(GROUP):
        att_ref[n] = att[n * block : (n + 1) * block, :].astype(BF16)


def shards(queries, latent, grad_out, doc_start, block_list):
    list_width = block_list.shape[1]
    block, heads, width = queries.shape
    latent_width = grad_out.shape[2]
    scale = 1.0 / math.sqrt(latent_width // 4 + width - latent_width)
    ctx = lax.axis_index("ctx").astype(jnp.int32)
    keys = list_width * block
    steps = heads // GROUP
    rows = GROUP * block

    latent_t = latent.T
    window = [shifted(latent_t, "ctx", d) for d in range(list_width - 1, 0, -1)] + [latent_t]
    q_t = queries.transpose(1, 2, 0)
    g_t = grad_out.transpose(1, 2, 0)

    whole = lambda shape: pl.BlockSpec(shape, lambda i: (0,) * len(shape))
    by_step = lambda *tail: pl.BlockSpec((1, *tail), lambda i: (i,) + (0,) * len(tail))
    by_group = lambda *tail: pl.BlockSpec((GROUP, *tail), lambda i: (i,) + (0,) * len(tail))
    smem = pl.BlockSpec(memory_space=pltpu.SMEM)
    weight, grad_score, partial = pl.pallas_call(
        functools.partial(backward_kernel, scale),
        grid=(steps,),
        in_specs=[smem, smem, whole((1, block))]
        + [whole((width, block))] * list_width
        + [by_group(width, block), by_group(latent_width, block)],
        out_specs=[by_step(keys, rows), by_step(keys, rows), whole((width, keys))],
        out_shape=[
            jax.ShapeDtypeStruct((steps, keys, rows), BF16),
            jax.ShapeDtypeStruct((steps, keys, rows), BF16),
            jax.ShapeDtypeStruct((width, keys), BF16),
        ],
        scratch_shapes=[
            pltpu.VMEM((keys, width), BF16),
            pltpu.VMEM((keys, block), F32),
            pltpu.VMEM((width, keys), F32),
        ],
        compiler_params=pltpu.CompilerParams(vmem_limit_bytes=40 << 20),
        cost_estimate=pl.CostEstimate(
            flops=2 * heads * block * keys * 2 * (width + latent_width),
            bytes_accessed=12 << 20,
            transcendentals=heads * block * keys,
        ),
        name="backward",
    )(ctx.reshape(1), block_list, doc_start.reshape(1, block), *window, q_t, g_t)

    head = lax.axis_index("head")
    parts = lax.axis_size("head")
    share = width // parts
    pieces = partial.reshape(parts, share, keys)
    piece = lambda n: lax.dynamic_index_in_dim(pieces, (head + n) % parts, 0, keepdims=False)
    arrived = [shifted(piece(n), "head", n) for n in range(1, parts)]
    own = piece(0).astype(F32)
    for part in arrived:
        own = own + part.astype(F32)
    total = own[:, keys - block :]
    for d in range(1, list_width):
        first = keys - (d + 1) * block
        total = total + shifted(own[:, first : first + block].astype(BF16), "ctx", -d).astype(F32)

    att, gq = pl.pallas_call(
        forward_kernel,
        grid=(steps,),
        in_specs=[whole((width, block))] * list_width + [by_step(keys, rows), by_step(keys, rows)],
        out_specs=[by_group(block, latent_width), by_group(width, block)],
        out_shape=[
            jax.ShapeDtypeStruct((heads, block, latent_width), BF16),
            jax.ShapeDtypeStruct((heads, width, block), F32),
        ],
        scratch_shapes=[pltpu.VMEM((width, keys), BF16), pltpu.VMEM((keys, latent_width), BF16)],
        compiler_params=pltpu.CompilerParams(vmem_limit_bytes=40 << 20),
        cost_estimate=pl.CostEstimate(
            flops=2 * heads * block * keys * (width + latent_width),
            bytes_accessed=12 << 20,
            transcendentals=0,
        ),
        name="forward",
    )(*window, weight, grad_score)
    return (att.transpose(1, 0, 2), gq.transpose(2, 0, 1), total.T)


def solution(mesh):
    placed = (
        P("ctx", "head", None),
        P("ctx", None),
        P("ctx", "head", None),
        P("ctx"),
        P("ctx", None),
    )
    return jax.shard_map(
        shards,
        mesh=mesh,
        in_specs=placed,
        out_specs=(P("ctx", "head", None), P("ctx", "head", None), P("ctx", "head")),
        check_vma=False,
    )
```

```python
import functools
import math

import jax
import jax.numpy as jnp
from jax import lax
from jax.experimental import pallas as pl
from jax.experimental.pallas import tpu as pltpu
from jax.sharding import PartitionSpec as P

F32 = jnp.float32
BF16 = jnp.bfloat16
SLOTS = 4
GROUP = 8
PART = 4
MIB = 1 << 20
NN = (((1,), (0,)), ((), ()))
NT = (((1,), (1,)), ((), ()))


def moved(value, axis, target):
    count = lax.axis_size(axis)
    return lax.ppermute(value, axis, [(s, target(s) % count) for s in range(count)])


def dot(a, b, dims=NN):
    return lax.dot_general(a, b, dims, preferred_element_type=F32)


def lanes(ref, first, count):
    return jnp.concatenate([ref[first + n] for n in range(count)], axis=1)


def fetch_kernel(q_ref, after_ref, out_ref, sems):
    del after_ref
    chunks = sems.shape[0]
    size = q_ref.shape[0] // chunks
    copies = [
        pltpu.make_async_copy(
            q_ref.at[pl.ds(n * size, size)], out_ref.at[pl.ds(n * size, size)], sems.at[n]
        )
        for n in range(chunks)
    ]
    for copy in copies:
        copy.start()
    for copy in copies:
        copy.wait()


def backward_kernel(scale, parts, place_ref, entries_ref, start_ref, *refs):
    key_refs = refs[:SLOTS]
    q_ref, g_ref, weight_ref, score_ref = refs[SLOTS : SLOTS + 4]
    piece_refs = refs[SLOTS + 4 : SLOTS + 4 + parts]
    rows_ref, bias_ref, acc_ref = refs[SLOTS + 4 + parts :]
    width, block = key_refs[0].shape
    heads, latent_width, _ = g_ref.shape
    place = place_ref[0]
    head = place_ref[1]

    parity = lax.rem(place, 2)
    offsets = (1 + 2 * parity, 3 - 2 * parity, 2, 0)
    q_pos = place * block + lax.broadcasted_iota(jnp.int32, (block, block), 1)
    q_start = start_ref[...]
    for slot in range(SLOTS):
        span = slice(slot * block, (slot + 1) * block)
        rows_ref[span, :] = key_refs[slot][...].T
        entry = place - offsets[slot]
        listed = entries_ref[0, 0] == entry
        for n in range(1, entries_ref.shape[1]):
            listed = listed | (entries_ref[0, n] == entry)
        listed = listed & (entry >= 0)
        first = jnp.where(listed, entry * block, 1 << 24)
        k_pos = first + lax.broadcasted_iota(jnp.int32, (block, block), 0)
        allowed = (k_pos <= q_pos) & (k_pos >= q_start)
        bias_ref[span, :] = jnp.where(allowed, 0.0, -1e30)

    bias = jnp.concatenate([bias_ref[...]] * GROUP, axis=1)
    for group in range(heads // GROUP):
        q_cols = lanes(q_ref, group * GROUP, GROUP)
        g_cols = lanes(g_ref, group * GROUP, GROUP)
        score = dot(rows_ref[...], q_cols) * (scale * math.log2(math.e)) + bias
        grad_weight = dot(rows_ref[:, :latent_width], g_cols)
        top = jnp.max(score, axis=0, keepdims=True)
        terms = jnp.exp2(score - top)
        weight = terms * (1.0 / jnp.sum(terms, axis=0, keepdims=True))
        delta = jnp.sum(weight * grad_weight, axis=0, keepdims=True)
        grad_score = ((weight * scale) * (grad_weight - delta)).astype(BF16)
        weight = weight.astype(BF16)
        size = PART * block
        for n in range(GROUP // PART):
            weight_ref[group * (GROUP // PART) + n] = weight[:, n * size : (n + 1) * size]
            score_ref[group * (GROUP // PART) + n] = grad_score[:, n * size : (n + 1) * size]
        from_score = dot(q_cols, grad_score, NT)
        from_weight = dot(g_cols, weight, NT)
        if group == 0:
            acc_ref[...] = from_score
        else:
            acc_ref[...] += from_score
        acc_ref[:latent_width, :] += from_weight

    share = width // parts
    for n, piece_ref in enumerate(piece_refs):
        first = pl.multiple_of(lax.rem(head + n, parts) * share, share)
        piece_ref[...] = acc_ref[pl.ds(first, share), :].astype(BF16)


def forward_kernel(*refs):
    key_refs = refs[:SLOTS]
    weight_ref, score_ref, att_ref, gq_ref, cols_ref, rows_ref = refs[SLOTS:]
    block = key_refs[0].shape[1]
    latent_width = att_ref.shape[2]
    step = pl.program_id(0)

    @pl.when(step == 0)
    def _():
        for slot, key_ref in enumerate(key_refs):
            cols_ref[:, slot * block : (slot + 1) * block] = key_ref[...]
            rows_ref[slot * block : (slot + 1) * block, :] = key_ref[:latent_width, :].T

    grad = dot(cols_ref[...], score_ref[step])
    for n in range(PART):
        gq_ref[n] = grad[:, n * block : (n + 1) * block]
    att = dot(weight_ref[step].T, rows_ref[...])
    for n in range(PART):
        att_ref[n] = att[n * block : (n + 1) * block, :].astype(BF16)


def merge_kernel(*refs):
    pieces = refs[:-5]
    swap_ref, cross_ref, back_ref, own_ref = refs[-4:]
    total = pieces[0][...].astype(F32)
    for piece in pieces[1:]:
        total = total + piece[...].astype(F32)
    block = own_ref.shape[1]
    swap_ref[...] = total[:, :block].astype(BF16)
    cross_ref[...] = total[:, block : 2 * block].astype(BF16)
    back_ref[...] = total[:, 2 * block : 3 * block]
    own_ref[...] = total[:, 3 * block :]


def add_kernel(*refs):
    total = refs[0][...]
    for ref in refs[1:-1]:
        total = total + ref[...].astype(F32)
    refs[-1][...] = total.astype(refs[-1].dtype)


def shards(queries, latent, grad_out, doc_start, block_list):
    block, heads, width = queries.shape
    latent_width = grad_out.shape[2]
    scale = 1.0 / math.sqrt(latent_width // 4 + width - latent_width)
    parts = lax.axis_size("head")
    share = width // parts
    keys = SLOTS * block
    steps = heads // PART
    rows = PART * block
    place = jnp.stack([lax.axis_index("ctx"), lax.axis_index("head")]).astype(jnp.int32)
    vmem = pl.BlockSpec(memory_space=pltpu.VMEM)
    smem = pl.BlockSpec(memory_space=pltpu.SMEM)
    anywhere = pl.BlockSpec(memory_space=pl.ANY)
    keep = lambda x: pltpu.with_memory_space_constraint(x, pltpu.VMEM)
    limit = lambda n: pltpu.CompilerParams(vmem_limit_bytes=n * MIB)

    latent_t = latent.T
    crossed = moved(latent_t, "ctx", lambda s: s + 3 if s % 2 else s + 1)
    back = moved(latent_t, "ctx", lambda s: s + 2)
    g_t = grad_out.transpose(1, 2, 0)
    back, g_t = lax.optimization_barrier((back, g_t))
    swapped = moved(back, "ctx", lambda s: s ^ 1)
    window = [swapped, crossed, back, latent_t]

    q_t = pl.pallas_call(
        fetch_kernel,
        in_specs=[anywhere, anywhere],
        out_specs=vmem,
        out_shape=pltpu.VMEM((heads, width, block), BF16),
        scratch_shapes=[pltpu.SemaphoreType.DMA((8,))],
        compiler_params=limit(1),
        name="fetch",
    )(pltpu.with_memory_space_constraint(queries.transpose(1, 2, 0), pltpu.HBM), g_t)

    weight, grad_score, *pieces = pl.pallas_call(
        functools.partial(backward_kernel, scale, parts),
        in_specs=[smem, smem] + [vmem] * (SLOTS + 3),
        out_specs=[vmem] * (2 + parts),
        out_shape=[pltpu.VMEM((steps, keys, rows), BF16)] * 2
        + [jax.ShapeDtypeStruct((share, keys), BF16)] * parts,
        scratch_shapes=[
            pltpu.VMEM((keys, width), BF16),
            pltpu.VMEM((keys, block), F32),
            pltpu.VMEM((width, keys), F32),
        ],
        compiler_params=limit(20),
        cost_estimate=pl.CostEstimate(
            flops=2 * heads * block * keys * 2 * (width + latent_width),
            bytes_accessed=12 * MIB,
            transcendentals=heads * block * keys,
        ),
        name="backward",
    )(place, block_list, doc_start.reshape(1, block), *window, keep(q_t), g_t)

    arrived = [
        moved(piece, "head", lambda s, n=n: s + n) for n, piece in enumerate(pieces) if n
    ]

    by_group = lambda *tail: pl.BlockSpec((PART, *tail), lambda i: (i,) + (0,) * len(tail))
    att, gq = pl.pallas_call(
        forward_kernel,
        grid=(steps,),
        in_specs=[vmem] * (SLOTS + 2),
        out_specs=[by_group(block, latent_width), by_group(width, block)],
        out_shape=[
            jax.ShapeDtypeStruct((heads, block, latent_width), BF16),
            jax.ShapeDtypeStruct((heads, width, block), F32),
        ],
        scratch_shapes=[pltpu.VMEM((width, keys), BF16), pltpu.VMEM((keys, latent_width), BF16)],
        compiler_params=limit(20),
        cost_estimate=pl.CostEstimate(
            flops=2 * heads * block * keys * (width + latent_width),
            bytes_accessed=12 * MIB,
            transcendentals=0,
        ),
        name="forward",
    )(*window, keep(weight), keep(grad_score))

    to_swap, to_cross, to_back, own = pl.pallas_call(
        merge_kernel,
        in_specs=[vmem] * parts + [anywhere],
        out_specs=[vmem] * 4,
        out_shape=[jax.ShapeDtypeStruct((share, block), t) for t in (BF16, BF16, F32, F32)],
        compiler_params=limit(4),
        name="merge",
    )(pieces[0], *arrived, att)
    from_swap = moved(to_swap, "ctx", lambda s: s ^ 1)
    from_cross = moved(to_cross, "ctx", lambda s: s - 1 if s % 2 else s - 3)
    to_back = pl.pallas_call(
        add_kernel,
        in_specs=[vmem] * 2,
        out_specs=vmem,
        out_shape=jax.ShapeDtypeStruct((share, block), BF16),
        compiler_params=limit(1),
        name="add",
    )(to_back, from_swap)
    from_back = moved(to_back, "ctx", lambda s: s - 2)
    total = pl.pallas_call(
        add_kernel,
        in_specs=[vmem] * 3,
        out_specs=vmem,
        out_shape=jax.ShapeDtypeStruct((share, block), F32),
        compiler_params=limit(1),
        name="total",
    )(own, from_cross, from_back)
    return (att.transpose(1, 0, 2), gq.transpose(2, 0, 1), total.T)


def solution(mesh):
    placed = (
        P("ctx", "head", None),
        P("ctx", None),
        P("ctx", "head", None),
        P("ctx"),
        P("ctx", None),
    )
    return jax.shard_map(
        shards,
        mesh=mesh,
        in_specs=placed,
        out_specs=(P("ctx", "head", None), P("ctx", "head", None), P("ctx", "head")),
        check_vma=False,
    )
```

```python
import functools
import math

import jax
import jax.numpy as jnp
from jax import lax
from jax.experimental import pallas as pl
from jax.experimental.pallas import tpu as pltpu
from jax.sharding import PartitionSpec as P

F32 = jnp.float32
BF16 = jnp.bfloat16
SLOTS = 4
PART = 4
MIB = 1 << 20
NN = (((1,), (0,)), ((), ()))
NT = (((1,), (1,)), ((), ()))


def moved(value, axis, target):
    count = lax.axis_size(axis)
    return lax.ppermute(value, axis, [(s, target(s) % count) for s in range(count)])


def dot(a, b, dims=NN):
    return lax.dot_general(a, b, dims, preferred_element_type=F32)


def lanes(ref):
    return jnp.concatenate([ref[n] for n in range(ref.shape[0])], axis=1)


def mask_kernel(entries_ref, start_ref, mask_ref, token_ref):
    place = lax.axis_index("ctx")
    parity = lax.rem(place, 2)
    block = start_ref.shape[1]
    q_pos = place * block + lax.broadcasted_iota(jnp.int32, (block, block), 1)
    for slot, offset in enumerate((1 + 2 * parity, 3 - 2 * parity, 2, 0)):
        entry = place - offset
        listed = entries_ref[0, 0] == entry
        for n in range(1, entries_ref.shape[1]):
            listed = listed | (entries_ref[0, n] == entry)
        first = jnp.where(listed & (entry >= 0), entry * block, 1 << 24)
        k_pos = first + lax.broadcasted_iota(jnp.int32, (block, block), 0)
        allowed = (k_pos <= q_pos) & (k_pos >= start_ref[...])
        mask_ref[slot * block : (slot + 1) * block, :] = jnp.where(allowed, 0.0, -1e30)
    token_ref[...] = jnp.zeros_like(token_ref)


def scores_of(scale, keys, mask, q_cols, g_cols):
    heads = q_cols.shape[1] // mask.shape[1]
    mask = jnp.concatenate([mask] * heads, axis=1)
    score = dot(keys, q_cols) * (scale * math.log2(math.e)) + mask
    return score, dot(keys[:, : g_cols.shape[0]], g_cols)


def own_kernel(
    scale, mask_ref, key_ref, g_ref, from_ref, _, score_ref, grad_ref, q_ref, token_ref, sems
):
    chunks = sems.shape[0]
    size = from_ref.shape[0] // chunks
    copies = [
        pltpu.make_async_copy(
            from_ref.at[pl.ds(n * size, size)], q_ref.at[pl.ds(n * size, size)], sems.at[n]
        )
        for n in range(chunks)
    ]
    for copy in copies:
        copy.start()
    keys = key_ref[...].T
    first = mask_ref.shape[0] - keys.shape[0]
    mask = mask_ref[first:, :]
    span = size * mask.shape[1]
    for n, copy in enumerate(copies):
        copy.wait()
        heads = slice(n * size, (n + 1) * size)
        score, grad_weight = scores_of(scale, keys, mask, lanes(q_ref[heads]), lanes(g_ref[heads]))
        score_ref[:, n * span : (n + 1) * span] = score
        grad_ref[:, n * span : (n + 1) * span] = grad_weight
    token_ref[...] = jnp.zeros_like(token_ref)


def back_kernel(scale, mask_ref, key_ref, g_ref, q_ref, _, score_ref, grad_ref):
    block = key_ref.shape[1]
    mask = mask_ref[2 * block : 3 * block, :]
    score, grad_weight = scores_of(scale, key_ref[...].T, mask, lanes(q_ref), lanes(g_ref))
    score_ref[...] = score
    grad_ref[...] = grad_weight


def weights_kernel(scale, mask_ref, *refs):
    swap_ref, cross_ref, q_ref, g_ref, *known, weight_ref, score_ref, out_ref, grad_ref = refs
    keys = jnp.concatenate([swap_ref[...].T, cross_ref[...].T], axis=0)
    mask = mask_ref[: keys.shape[0], :]
    q_cols = lanes(q_ref)
    g_cols = lanes(g_ref)
    parts = [scores_of(scale, keys, mask, q_cols, g_cols)]
    parts += [(known[n][...], known[n + 1][...]) for n in range(0, len(known), 2)]
    top = functools.reduce(jnp.maximum, [jnp.max(s, axis=0, keepdims=True) for s, _ in parts])
    terms = [jnp.exp2(s - top) for s, _ in parts]
    total = sum(jnp.sum(t, axis=0, keepdims=True) for t in terms)
    inverse = 1.0 / total
    delta = inverse * sum(
        jnp.sum(t * g, axis=0, keepdims=True) for t, (_, g) in zip(terms, parts, strict=True)
    )
    size = weight_ref.shape[2]
    first = 0
    for t, (_, grad_weight) in zip(terms, parts, strict=True):
        weight = t * inverse
        grad_score = (weight * (grad_weight - delta)).astype(BF16)
        weight = weight.astype(BF16)
        if first == 0:
            width = g_cols.shape[0]
            grad_ref[...] = dot(q_cols, grad_score, NT) * scale
            grad_ref[:width, :] += dot(g_cols, weight, NT)
            out_ref[...] = grad_ref[...].astype(BF16)
        last = first + t.shape[0]
        for n in range(weight_ref.shape[0]):
            weight_ref[n, first:last, :] = weight[:, n * size : (n + 1) * size]
            score_ref[n, first:last, :] = grad_score[:, n * size : (n + 1) * size]
        first = last


def keys_kernel(scale, q_ref, g_ref, weight_ref, score_ref, grad_ref):
    first = weight_ref.shape[1] // 2
    steps = range(weight_ref.shape[0])
    width = g_ref.shape[1]
    grad_score = jnp.concatenate([score_ref[n, first:, :] for n in steps], axis=1)
    weight = jnp.concatenate([weight_ref[n, first:, :] for n in steps], axis=1)
    grad_ref[...] = dot(lanes(q_ref), grad_score, NT) * scale
    grad_ref[:width, :] += dot(lanes(g_ref), weight, NT)


def split_kernel(kept_ref, swap_ref, *refs):
    piece_refs = refs[:-1]
    total_ref = refs[-1]
    parts = len(piece_refs)
    block = kept_ref.shape[1] // 2
    odd = lax.rem(lax.axis_index("ctx"), 2) == 1
    crossed = swap_ref[:, block:].astype(F32)
    total_ref[:, :block] = jnp.where(odd, crossed, 0.0)
    total_ref[:, block : 2 * block] = kept_ref[:, :block] + swap_ref[:, :block].astype(F32)
    total_ref[:, 2 * block :] = kept_ref[:, block:] + jnp.where(odd, 0.0, crossed)
    share = total_ref.shape[0] // parts
    for n, piece_ref in enumerate(piece_refs):
        first = pl.multiple_of(lax.rem(lax.axis_index("head") + n, parts) * share, share)
        piece_ref[...] = total_ref[pl.ds(first, share), :].astype(piece_ref.dtype)


def forward_kernel(scale, *refs):
    key_refs = refs[:SLOTS]
    weight_ref, score_ref, att_ref, gq_ref, cols_ref, rows_ref = refs[SLOTS:]
    block = key_refs[0].shape[1]
    latent_width = att_ref.shape[2]
    step = pl.program_id(0)

    @pl.when(step == 0)
    def _():
        for slot, key_ref in enumerate(key_refs):
            cols_ref[:, slot * block : (slot + 1) * block] = key_ref[...]
            rows_ref[slot * block : (slot + 1) * block, :] = key_ref[:latent_width, :].T

    grad = dot(cols_ref[...], score_ref[step]) * scale
    for n in range(PART):
        gq_ref[n] = grad[:, n * block : (n + 1) * block]
    att = dot(weight_ref[step].T, rows_ref[...])
    for n in range(PART):
        att_ref[n] = att[n * block : (n + 1) * block, :].astype(BF16)


def merge_kernel(own_ref, *refs):
    far_ref, back_ref, rest_ref = refs[-3:]
    total = own_ref[...]
    for ref in refs[:-4]:
        total = total + ref[...].astype(F32)
    block = rest_ref.shape[1]
    far_ref[...] = total[:, :block].astype(BF16)
    back_ref[...] = total[:, block : 2 * block].astype(BF16)
    rest_ref[...] = total[:, 2 * block :]


def add_kernel(*refs):
    total = refs[0][...]
    for ref in refs[1:-1]:
        total = total + ref[...].astype(F32)
    refs[-1][...] = total.astype(refs[-1].dtype)


def shards(queries, latent, grad_out, doc_start, block_list):
    block, heads, width = queries.shape
    latent_width = grad_out.shape[2]
    scale = 1.0 / math.sqrt(latent_width // 4 + width - latent_width)
    parts = lax.axis_size("head")
    share = width // parts
    keys = SLOTS * block
    steps = heads // PART
    rows = PART * block
    vmem = pl.BlockSpec(memory_space=pltpu.VMEM)
    smem = pl.BlockSpec(memory_space=pltpu.SMEM)
    anywhere = pl.BlockSpec(memory_space=pl.ANY)
    keep = lambda x: pltpu.with_memory_space_constraint(x, pltpu.VMEM)
    limit = lambda n: pltpu.CompilerParams(vmem_limit_bytes=n * MIB)

    latent_t = latent.T
    back = moved(latent_t, "ctx", lambda s: s + 2)
    mask, token = pl.pallas_call(
        mask_kernel,
        in_specs=[smem, vmem],
        out_specs=[vmem] * 2,
        out_shape=[pltpu.VMEM((keys, block), F32), jax.ShapeDtypeStruct((8, 128), F32)],
        compiler_params=limit(2),
        name="mask",
    )(block_list, doc_start.reshape(1, block))
    mask = keep(mask)
    latent_c, token = lax.optimization_barrier((latent_t, token))
    crossed = moved(latent_c, "ctx", lambda s: s + 3 if s % 2 else s + 1)

    g_t = keep(grad_out.transpose(1, 2, 0))
    block_cost = pl.CostEstimate(
        flops=2 * heads * block * block * (width + latent_width),
        bytes_accessed=4 * MIB,
        transcendentals=0,
    )
    own_score, own_grad, q_t, token = pl.pallas_call(
        functools.partial(own_kernel, scale),
        in_specs=[vmem] * 3 + [anywhere] * 2,
        out_specs=[vmem] * 4,
        out_shape=[pltpu.VMEM((block, heads * block), F32)] * 2
        + [pltpu.VMEM((heads, width, block), BF16), jax.ShapeDtypeStruct((8, 128), F32)],
        scratch_shapes=[pltpu.SemaphoreType.DMA((heads // PART,))],
        compiler_params=limit(16),
        cost_estimate=block_cost,
        name="own",
    )(
        mask,
        keep(latent_t),
        g_t,
        pltpu.with_memory_space_constraint(queries.transpose(1, 2, 0), pltpu.HBM),
        token,
    )
    own_score, own_grad, q_t = keep(own_score), keep(own_grad), keep(q_t)
    back, token = lax.optimization_barrier((back, token))
    swapped = moved(back, "ctx", lambda s: s ^ 1)
    back_score, back_grad = pl.pallas_call(
        functools.partial(back_kernel, scale),
        in_specs=[vmem] * 4 + [anywhere],
        out_specs=[vmem] * 2,
        out_shape=[pltpu.VMEM((block, heads * block), F32)] * 2,
        compiler_params=limit(16),
        cost_estimate=block_cost,
        name="back",
    )(mask, keep(back), g_t, q_t, token)
    back_score, back_grad = keep(back_score), keep(back_grad)
    window = [keep(swapped), keep(crossed), keep(back), keep(latent_t)]

    weight, grad_score, to_swap = pl.pallas_call(
        functools.partial(weights_kernel, scale),
        in_specs=[vmem] * 9,
        out_specs=[vmem] * 3,
        out_shape=[pltpu.VMEM((steps, keys, rows), BF16)] * 2
        + [pltpu.VMEM((width, keys // 2), BF16)],
        scratch_shapes=[pltpu.VMEM((width, keys // 2), F32)],
        compiler_params=limit(28),
        cost_estimate=pl.CostEstimate(
            flops=2 * heads * block * keys * (width + latent_width),
            bytes_accessed=12 * MIB,
            transcendentals=heads * block * keys,
        ),
        name="weights",
    )(mask, *window[:2], q_t, g_t, back_score, back_grad, own_score, own_grad)
    weight, grad_score = keep(weight), keep(grad_score)
    from_swap = moved(to_swap, "ctx", lambda s: s ^ 1)

    kept = pl.pallas_call(
        functools.partial(keys_kernel, scale),
        in_specs=[vmem] * 4,
        out_specs=vmem,
        out_shape=pltpu.VMEM((width, keys // 2), F32),
        compiler_params=limit(16),
        cost_estimate=pl.CostEstimate(
            flops=heads * block * keys * (width + latent_width),
            bytes_accessed=8 * MIB,
            transcendentals=0,
        ),
        name="keys",
    )(q_t, g_t, weight, grad_score)

    own, *pieces = pl.pallas_call(
        split_kernel,
        in_specs=[vmem] * 2,
        out_specs=[vmem] * parts,
        out_shape=[
            pltpu.VMEM((share, 3 * block), BF16 if n else F32) for n in range(parts)
        ],
        scratch_shapes=[pltpu.VMEM((width, 3 * block), F32)],
        compiler_params=limit(4),
        name="split",
    )(keep(kept), keep(from_swap))
    arrived = [moved(piece, "head", lambda s, n=n: s + n + 1) for n, piece in enumerate(pieces)]

    by_group = lambda *tail: pl.BlockSpec((PART, *tail), lambda i: (i,) + (0,) * len(tail))
    att, gq = pl.pallas_call(
        functools.partial(forward_kernel, scale),
        grid=(steps,),
        in_specs=[vmem] * (SLOTS + 2),
        out_specs=[by_group(block, latent_width), by_group(width, block)],
        out_shape=[
            jax.ShapeDtypeStruct((heads, block, latent_width), BF16),
            jax.ShapeDtypeStruct((heads, width, block), F32),
        ],
        scratch_shapes=[pltpu.VMEM((width, keys), BF16), pltpu.VMEM((keys, latent_width), BF16)],
        compiler_params=limit(20),
        cost_estimate=pl.CostEstimate(
            flops=2 * heads * block * keys * (width + latent_width),
            bytes_accessed=12 * MIB,
            transcendentals=0,
        ),
        name="forward",
    )(*window, weight, grad_score)

    to_far, to_back, rest = pl.pallas_call(
        merge_kernel,
        in_specs=[vmem] * parts + [anywhere],
        out_specs=[vmem] * 3,
        out_shape=[pltpu.VMEM((share, block), t) for t in (BF16, BF16, F32)],
        compiler_params=limit(4),
        name="merge",
    )(keep(own), *map(keep, arrived), att)
    from_back = moved(to_back, "ctx", lambda s: s - 2)
    from_far = moved(to_far, "ctx", lambda s: s - 4)
    total = pl.pallas_call(
        add_kernel,
        in_specs=[vmem] * 3,
        out_specs=vmem,
        out_shape=jax.ShapeDtypeStruct((share, block), F32),
        compiler_params=limit(1),
        name="total",
    )(*map(keep, (rest, from_back, from_far)))
    return (att.transpose(1, 0, 2), gq.transpose(2, 0, 1), total.T)


def solution(mesh):
    placed = (
        P("ctx", "head", None),
        P("ctx", None),
        P("ctx", "head", None),
        P("ctx"),
        P("ctx", None),
    )
    return jax.shard_map(
        shards,
        mesh=mesh,
        in_specs=placed,
        out_specs=(P("ctx", "head", None), P("ctx", "head", None), P("ctx", "head")),
        check_vma=False,
    )
```

```python
import functools
import math

import jax
import jax.numpy as jnp
from jax import lax
from jax.experimental import pallas as pl
from jax.experimental.pallas import tpu as pltpu
from jax.sharding import PartitionSpec as P

F32 = jnp.float32
BF16 = jnp.bfloat16
SLOTS = 4
PART = 4
COPIES = (4, 2)
MIB = 1 << 20
NN = (((1,), (0,)), ((), ()))
NT = (((1,), (1,)), ((), ()))


def moved(value, axis, target):
    count = lax.axis_size(axis)
    return lax.ppermute(value, axis, [(s, target(s) % count) for s in range(count)])


def dot(a, b, dims=NN):
    return lax.dot_general(a, b, dims, preferred_element_type=F32)


def lanes(ref):
    return jnp.concatenate([ref[n] for n in range(ref.shape[0])], axis=1)


def write_mask(mask_ref, entries_ref, start_ref):
    place = lax.axis_index("ctx")
    parity = lax.rem(place, 2)
    block = start_ref.shape[1]
    q_pos = place * block + lax.broadcasted_iota(jnp.int32, (block, block), 1)
    for slot, offset in enumerate((1 + 2 * parity, 3 - 2 * parity, 2, 0)):
        entry = place - offset
        listed = entries_ref[0, 0] == entry
        for n in range(1, entries_ref.shape[1]):
            listed = listed | (entries_ref[0, n] == entry)
        first = jnp.where(listed & (entry >= 0), entry * block, 1 << 24)
        k_pos = first + lax.broadcasted_iota(jnp.int32, (block, block), 0)
        allowed = (k_pos <= q_pos) & (k_pos >= start_ref[...])
        mask_ref[slot * block : (slot + 1) * block, :] = jnp.where(allowed, 0.0, -1e30)


def scores_of(scale, keys, mask, q_cols):
    heads = q_cols.shape[1] // mask.shape[1]
    mask = jnp.concatenate([mask] * heads, axis=1)
    return dot(keys, q_cols) * (scale * math.log2(math.e)) + mask


def own_kernel(scale, key_from, entries_from, start_from, g_from, q_from, *refs):
    score_ref, grad_ref, q_ref, g_ref, mask_ref, key_ref, token_ref = refs[:7]
    entries_ref, start_ref, buffer_ref, sems = refs[7:]
    tokens, heads, latent_width = g_from.shape
    g_chunks, q_chunks = COPIES
    tables = [
        pltpu.make_async_copy(entries_from, entries_ref, sems.at[0]),
        pltpu.make_async_copy(start_from, start_ref, sems.at[1]),
        pltpu.make_async_copy(key_from, key_ref, sems.at[2]),
    ]
    size = tokens // g_chunks
    g_copies = [
        pltpu.make_async_copy(
            g_from.at[pl.ds(n * size, size)], buffer_ref.at[pl.ds(n * size, size)], sems.at[3 + n]
        )
        for n in range(g_chunks)
    ]
    part_heads = heads // q_chunks
    q_copies = [
        pltpu.make_async_copy(
            q_from.at[pl.ds(n * part_heads, part_heads)],
            q_ref.at[pl.ds(n * part_heads, part_heads)],
            sems.at[3 + g_chunks + n],
        )
        for n in range(q_chunks)
    ]
    for copy in tables + g_copies + q_copies:
        copy.start()
    token_ref[...] = jnp.zeros_like(token_ref)
    for copy in tables:
        copy.wait()
    keys = key_ref[...].T
    write_mask(mask_ref, entries_ref, start_ref)
    mask = mask_ref[mask_ref.shape[0] - keys.shape[0] :, :]

    few = 256 // heads
    order = regroup(few, heads)
    for n, copy in enumerate(g_copies):
        copy.wait()
        for first in range(n * size, (n + 1) * size, few):
            part = buffer_ref[first : first + few].reshape(few * heads, latent_width)
            part = dot(order, part).astype(BF16)
            for h in range(heads):
                g_ref[h * tokens + first : h * tokens + first + few, :] = part[
                    h * few : (h + 1) * few
                ]
    grad_ref[...] = dot(keys[:, :latent_width], g_ref[...], NT)
    span = part_heads * tokens
    for n, copy in enumerate(q_copies):
        copy.wait()
        q_cols = lanes(q_ref[n * part_heads : (n + 1) * part_heads])
        score_ref[:, n * span : (n + 1) * span] = scores_of(scale, keys, mask, q_cols)


def back_kernel(scale, mask_ref, key_ref, q_ref, g_ref, _, score_ref, grad_ref):
    block = key_ref.shape[1]
    mask = mask_ref[2 * block : 3 * block, :]
    keys = key_ref[...].T
    score_ref[...] = scores_of(scale, keys, mask, lanes(q_ref))
    grad_ref[...] = dot(keys[:, : g_ref.shape[1]], g_ref[...], NT)


def weights_kernel(scale, mask_ref, *refs):
    swap_ref, cross_ref, q_ref, g_ref, *known, weight_ref, score_ref, out_ref, grad_ref = refs
    keys = jnp.concatenate([swap_ref[...].T, cross_ref[...].T], axis=0)
    mask = mask_ref[: keys.shape[0], :]
    q_cols = lanes(q_ref)
    width = g_ref.shape[1]
    parts = [(scores_of(scale, keys, mask, q_cols), dot(keys[:, :width], g_ref[...], NT))]
    parts += [(known[n][...], known[n + 1][...]) for n in range(0, len(known), 2)]
    top = functools.reduce(jnp.maximum, [jnp.max(s, axis=0, keepdims=True) for s, _ in parts])
    terms = [jnp.exp2(s - top) for s, _ in parts]
    total = sum(jnp.sum(t, axis=0, keepdims=True) for t in terms)
    inverse = 1.0 / total
    delta = inverse * sum(
        jnp.sum(t * g, axis=0, keepdims=True) for t, (_, g) in zip(terms, parts, strict=True)
    )
    size = weight_ref.shape[2]
    first = 0
    for t, (_, grad_weight) in zip(terms, parts, strict=True):
        weight = t * inverse
        grad_score = (weight * (grad_weight - delta)).astype(BF16)
        weight = weight.astype(BF16)
        if first == 0:
            grad_ref[...] = dot(q_cols, grad_score, NT) * scale
            grad_ref[:width, :] += dot(weight, g_ref[...]).T
            out_ref[...] = grad_ref[...].astype(BF16)
        last = first + t.shape[0]
        for n in range(weight_ref.shape[0]):
            weight_ref[n, first:last, :] = weight[:, n * size : (n + 1) * size]
            score_ref[n, first:last, :] = grad_score[:, n * size : (n + 1) * size]
        first = last


def keys_kernel(scale, q_ref, g_ref, weight_ref, score_ref, grad_ref):
    first = weight_ref.shape[1] // 2
    steps = range(weight_ref.shape[0])
    width = g_ref.shape[1]
    grad_score = jnp.concatenate([score_ref[n, first:, :] for n in steps], axis=1)
    weight = jnp.concatenate([weight_ref[n, first:, :] for n in steps], axis=1)
    grad_ref[...] = dot(lanes(q_ref), grad_score, NT) * scale
    grad_ref[:width, :] += dot(weight, g_ref[...]).T


def split_kernel(kept_ref, swap_ref, *refs):
    piece_refs = refs[:-1]
    total_ref = refs[-1]
    parts = len(piece_refs)
    block = kept_ref.shape[1] // 2
    odd = lax.rem(lax.axis_index("ctx"), 2) == 1
    crossed = swap_ref[:, block:].astype(F32)
    total_ref[:, :block] = jnp.where(odd, crossed, 0.0)
    total_ref[:, block : 2 * block] = kept_ref[:, :block] + swap_ref[:, :block].astype(F32)
    total_ref[:, 2 * block :] = kept_ref[:, block:] + jnp.where(odd, 0.0, crossed)
    share = total_ref.shape[0] // parts
    for n, piece_ref in enumerate(piece_refs):
        first = pl.multiple_of(lax.rem(lax.axis_index("head") + n, parts) * share, share)
        piece_ref[...] = total_ref[pl.ds(first, share), :].astype(piece_ref.dtype)


def regroup(few, heads):
    row = lax.broadcasted_iota(jnp.int32, (few * heads, few * heads), 0)
    col = lax.broadcasted_iota(jnp.int32, (few * heads, few * heads), 1)
    order = (row // few == col % heads) & (row % few == col // heads)
    return order.astype(F32).astype(BF16)


def forward_kernel(scale, *refs):
    key_refs = refs[:SLOTS]
    weight_ref, score_ref, att_to, gq_to, cols_ref, rows_ref = refs[SLOTS : SLOTS + 6]
    by_head_ref, att_ref, gq_ref, sems = refs[SLOTS + 6 :]
    block = key_refs[0].shape[1]
    tokens, heads, latent_width = att_ref.shape
    steps = heads // PART
    copies = []

    def send(source, target, first, count):
        span = pl.ds(first, count)
        copies.append(
            pltpu.make_async_copy(source.at[span], target.at[span], sems.at[len(copies)])
        )
        copies[-1].start()

    def grad_queries(step):
        grad = dot(cols_ref[...], score_ref[step]) * scale
        for n in range(PART):
            gq_ref[step * PART + n] = grad[:, n * block : (n + 1) * block]
        send(gq_ref, gq_to, step * PART, PART)

    for slot, key_ref in enumerate(key_refs):
        cols_ref[:, slot * block : (slot + 1) * block] = key_ref[...]
        rows_ref[slot * block : (slot + 1) * block, :] = key_ref[:latent_width, :].T
    grad_queries(0)
    span = PART * block
    for step in range(steps):
        att = dot(weight_ref[step].T, rows_ref[...])
        by_head_ref[step * span : (step + 1) * span, :] = att.astype(BF16)
    few = 256 // heads
    order = regroup(few, heads)
    size = tokens // steps
    for chunk in range(steps):
        for first in range(chunk * size, (chunk + 1) * size, few):
            part = jnp.concatenate(
                [by_head_ref[h * tokens + first : h * tokens + first + few, :] for h in range(heads)],
                axis=0,
            )
            part = lax.dot_general(
                order, part, (((0,), (0,)), ((), ())), preferred_element_type=F32
            )
            att_ref[first : first + few] = part.astype(BF16).reshape(few, heads, latent_width)
        send(att_ref, att_to, chunk * size, size)
    for step in range(1, steps):
        grad_queries(step)
    for copy in copies:
        copy.wait()


def merge_kernel(own_ref, *refs):
    far_ref, back_ref, rest_ref = refs[-3:]
    total = own_ref[...]
    for ref in refs[:-4]:
        total = total + ref[...].astype(F32)
    block = rest_ref.shape[1]
    far_ref[...] = total[:, :block].astype(BF16)
    back_ref[...] = total[:, block : 2 * block].astype(BF16)
    rest_ref[...] = total[:, 2 * block :]


def add_kernel(*refs):
    total = refs[0][...]
    for ref in refs[1:-1]:
        total = total + ref[...].astype(F32)
    refs[-1][...] = total.astype(refs[-1].dtype)


def shards(queries, latent, grad_out, doc_start, block_list):
    block, heads, width = queries.shape
    latent_width = grad_out.shape[2]
    scale = 1.0 / math.sqrt(latent_width // 4 + width - latent_width)
    parts = lax.axis_size("head")
    share = width // parts
    keys = SLOTS * block
    steps = heads // PART
    rows = PART * block
    vmem = pl.BlockSpec(memory_space=pltpu.VMEM)
    smem = pl.BlockSpec(memory_space=pltpu.SMEM)
    anywhere = pl.BlockSpec(memory_space=pl.ANY)
    keep = lambda x: pltpu.with_memory_space_constraint(x, pltpu.VMEM)
    limit = lambda n: pltpu.CompilerParams(vmem_limit_bytes=n * MIB)

    latent_t = latent.T
    back = moved(latent_t, "ctx", lambda s: s + 2)
    crossed = moved(latent_t, "ctx", lambda s: s + 3 if s % 2 else s + 1)

    block_cost = pl.CostEstimate(
        flops=2 * heads * block * block * (width + latent_width),
        bytes_accessed=4 * MIB,
        transcendentals=0,
    )
    in_hbm = lambda x: pltpu.with_memory_space_constraint(x, pltpu.HBM)
    own_score, own_grad, q_t, g_rows, mask, own_t, token = pl.pallas_call(
        functools.partial(own_kernel, scale),
        in_specs=[anywhere] * 5,
        out_specs=[vmem] * 7,
        out_shape=[pltpu.VMEM((block, heads * block), F32)] * 2
        + [
            pltpu.VMEM((heads, width, block), BF16),
            pltpu.VMEM((heads * block, latent_width), BF16),
            pltpu.VMEM((keys, block), F32),
            pltpu.VMEM((width, block), BF16),
            jax.ShapeDtypeStruct((8, 128), F32),
        ],
        scratch_shapes=[
            pltpu.SMEM(block_list.shape, jnp.int32),
            pltpu.VMEM((1, block), jnp.int32),
            pltpu.VMEM((block, heads, latent_width), BF16),
            pltpu.SemaphoreType.DMA((3 + sum(COPIES),)),
        ],
        compiler_params=limit(16),
        cost_estimate=block_cost,
        name="own",
    )(
        in_hbm(latent_t),
        in_hbm(block_list),
        in_hbm(doc_start.reshape(1, block)),
        in_hbm(grad_out),
        in_hbm(queries.transpose(1, 2, 0)),
    )
    g_rows, mask, own_t = keep(g_rows), keep(mask), keep(own_t)
    own_score, own_grad, q_t = keep(own_score), keep(own_grad), keep(q_t)
    back, token = lax.optimization_barrier((back, token))
    swapped = moved(back, "ctx", lambda s: s ^ 1)
    back_score, back_grad = pl.pallas_call(
        functools.partial(back_kernel, scale),
        in_specs=[vmem] * 4 + [anywhere],
        out_specs=[vmem] * 2,
        out_shape=[pltpu.VMEM((block, heads * block), F32)] * 2,
        compiler_params=limit(16),
        cost_estimate=block_cost,
        name="back",
    )(mask, keep(back), q_t, g_rows, token)
    back_score, back_grad = keep(back_score), keep(back_grad)
    window = [keep(swapped), keep(crossed), keep(back), own_t]

    weight, grad_score, to_swap = pl.pallas_call(
        functools.partial(weights_kernel, scale),
        in_specs=[vmem] * 9,
        out_specs=[vmem] * 3,
        out_shape=[pltpu.VMEM((steps, keys, rows), BF16)] * 2
        + [pltpu.VMEM((width, keys // 2), BF16)],
        scratch_shapes=[pltpu.VMEM((width, keys // 2), F32)],
        compiler_params=limit(28),
        cost_estimate=pl.CostEstimate(
            flops=2 * heads * block * keys * (width + latent_width),
            bytes_accessed=12 * MIB,
            transcendentals=heads * block * keys,
        ),
        name="weights",
    )(mask, *window[:2], q_t, g_rows, back_score, back_grad, own_score, own_grad)
    weight, grad_score = keep(weight), keep(grad_score)
    from_swap = moved(to_swap, "ctx", lambda s: s ^ 1)

    kept = pl.pallas_call(
        functools.partial(keys_kernel, scale),
        in_specs=[vmem] * 4,
        out_specs=vmem,
        out_shape=pltpu.VMEM((width, keys // 2), F32),
        compiler_params=limit(16),
        cost_estimate=pl.CostEstimate(
            flops=heads * block * keys * (width + latent_width),
            bytes_accessed=8 * MIB,
            transcendentals=0,
        ),
        name="keys",
    )(q_t, g_rows, weight, grad_score)

    own, *pieces = pl.pallas_call(
        split_kernel,
        in_specs=[vmem] * 2,
        out_specs=[vmem] * parts,
        out_shape=[
            pltpu.VMEM((share, 3 * block), BF16 if n else F32) for n in range(parts)
        ],
        scratch_shapes=[pltpu.VMEM((width, 3 * block), F32)],
        compiler_params=limit(4),
        name="split",
    )(keep(kept), keep(from_swap))
    arrived = [moved(piece, "head", lambda s, n=n: s + n + 1) for n, piece in enumerate(pieces)]

    att, gq = pl.pallas_call(
        functools.partial(forward_kernel, scale),
        in_specs=[vmem] * (SLOTS + 2),
        out_specs=[anywhere] * 2,
        out_shape=[
            pltpu.HBM((block, heads, latent_width), BF16),
            pltpu.HBM((heads, width, block), F32),
        ],
        scratch_shapes=[
            pltpu.VMEM((width, keys), BF16),
            pltpu.VMEM((keys, latent_width), BF16),
            pltpu.VMEM((heads * block, latent_width), BF16),
            pltpu.VMEM((block, heads, latent_width), BF16),
            pltpu.VMEM((heads, width, block), F32),
            pltpu.SemaphoreType.DMA((2 * steps,)),
        ],
        compiler_params=limit(28),
        cost_estimate=pl.CostEstimate(
            flops=2 * heads * block * keys * (width + latent_width),
            bytes_accessed=12 * MIB,
            transcendentals=0,
        ),
        name="forward",
    )(*window, weight, grad_score)

    to_far, to_back, rest = pl.pallas_call(
        merge_kernel,
        in_specs=[vmem] * parts + [anywhere],
        out_specs=[vmem] * 3,
        out_shape=[pltpu.VMEM((share, block), t) for t in (BF16, BF16, F32)],
        compiler_params=limit(4),
        name="merge",
    )(keep(own), *map(keep, arrived), in_hbm(att))
    from_back = moved(to_back, "ctx", lambda s: s - 2)
    from_far = moved(to_far, "ctx", lambda s: s - 4 if s % 2 else s - 2)
    total = pl.pallas_call(
        add_kernel,
        in_specs=[vmem] * 3,
        out_specs=vmem,
        out_shape=jax.ShapeDtypeStruct((share, block), F32),
        compiler_params=limit(1),
        name="total",
    )(*map(keep, (rest, from_back, from_far)))
    return (att, gq.transpose(2, 0, 1), total.T)


def solution(mesh):
    placed = (
        P("ctx", "head", None),
        P("ctx", None),
        P("ctx", "head", None),
        P("ctx"),
        P("ctx", None),
    )
    return jax.shard_map(
        shards,
        mesh=mesh,
        in_specs=placed,
        out_specs=(P("ctx", "head", None), P("ctx", "head", None), P("ctx", "head")),
        check_vma=False,
    )
```

```python
import functools
import math

import jax
import jax.numpy as jnp
from jax import lax
from jax.experimental import pallas as pl
from jax.experimental.pallas import tpu as pltpu
from jax.sharding import PartitionSpec as P

F32 = jnp.float32
BF16 = jnp.bfloat16
SLOTS = 4
PART = 4
COPIES = (4, 2)
MIB = 1 << 20
NN = (((1,), (0,)), ((), ()))
NT = (((1,), (1,)), ((), ()))


def moved(value, axis, target):
    count = lax.axis_size(axis)
    return lax.ppermute(value, axis, [(s, target(s) % count) for s in range(count)])


def dot(a, b, dims=NN):
    return lax.dot_general(a, b, dims, preferred_element_type=F32)


def lanes(ref):
    return jnp.concatenate([ref[n] for n in range(ref.shape[0])], axis=1)


def write_mask(mask_ref, entries_ref, start_ref):
    place = lax.axis_index("ctx")
    parity = lax.rem(place, 2)
    block = start_ref.shape[1]
    q_pos = place * block + lax.broadcasted_iota(jnp.int32, (block, block), 1)
    for slot, offset in enumerate((1 + 2 * parity, 3 - 2 * parity, 2, 0)):
        entry = place - offset
        listed = entries_ref[0, 0] == entry
        for n in range(1, entries_ref.shape[1]):
            listed = listed | (entries_ref[0, n] == entry)
        first = jnp.where(listed & (entry >= 0), entry * block, 1 << 24)
        k_pos = first + lax.broadcasted_iota(jnp.int32, (block, block), 0)
        allowed = (k_pos <= q_pos) & (k_pos >= start_ref[...])
        mask_ref[slot * block : (slot + 1) * block, :] = jnp.where(allowed, 0.0, -1e30)


def scores_of(scale, keys, mask, q_cols):
    heads = q_cols.shape[1] // mask.shape[1]
    mask = jnp.concatenate([mask] * heads, axis=1)
    return dot(keys, q_cols) * (scale * math.log2(math.e)) + mask


def partial_softmax(score, grad_weight, term_ref, stats_ref, span):
    top = jnp.max(score, axis=0, keepdims=True)
    terms = jnp.exp2(score - top)
    term_ref[:, span] = terms
    stats_ref[0:1, span] = top
    stats_ref[1:2, span] = jnp.sum(terms, axis=0, keepdims=True)
    stats_ref[2:3, span] = jnp.sum(terms * grad_weight, axis=0, keepdims=True)


def own_kernel(scale, key_from, entries_from, start_from, g_from, q_from, *refs):
    term_ref, grad_ref, stats_ref, q_ref, g_ref, mask_ref, key_ref, token_ref = refs[:8]
    entries_ref, start_ref, buffer_ref, sems = refs[8:]
    tokens, heads, latent_width = g_from.shape
    g_chunks, q_chunks = COPIES
    tables = [
        pltpu.make_async_copy(entries_from, entries_ref, sems.at[0]),
        pltpu.make_async_copy(start_from, start_ref, sems.at[1]),
        pltpu.make_async_copy(key_from, key_ref, sems.at[2]),
    ]
    size = tokens // g_chunks
    g_copies = [
        pltpu.make_async_copy(
            g_from.at[pl.ds(n * size, size)], buffer_ref.at[pl.ds(n * size, size)], sems.at[3 + n]
        )
        for n in range(g_chunks)
    ]
    part_heads = heads // q_chunks
    q_copies = [
        pltpu.make_async_copy(
            q_from.at[pl.ds(n * part_heads, part_heads)],
            q_ref.at[pl.ds(n * part_heads, part_heads)],
            sems.at[3 + g_chunks + n],
        )
        for n in range(q_chunks)
    ]
    for copy in tables + g_copies + q_copies:
        copy.start()
    token_ref[...] = jnp.zeros_like(token_ref)
    for copy in tables:
        copy.wait()
    keys = key_ref[...].T
    write_mask(mask_ref, entries_ref, start_ref)
    mask = mask_ref[mask_ref.shape[0] - keys.shape[0] :, :]

    few = 256 // heads
    order = regroup(few, heads)
    for n, copy in enumerate(g_copies):
        copy.wait()
        for first in range(n * size, (n + 1) * size, few):
            part = buffer_ref[first : first + few].reshape(few * heads, latent_width)
            part = dot(order, part).astype(BF16)
            for h in range(heads):
                g_ref[h * tokens + first : h * tokens + first + few, :] = part[
                    h * few : (h + 1) * few
                ]
    grad_ref[...] = dot(keys[:, :latent_width], g_ref[...], NT)
    span = part_heads * tokens
    for n, copy in enumerate(q_copies):
        copy.wait()
        q_cols = lanes(q_ref[n * part_heads : (n + 1) * part_heads])
        columns = slice(n * span, (n + 1) * span)
        score = scores_of(scale, keys, mask, q_cols)
        partial_softmax(score, grad_ref[:, columns], term_ref, stats_ref, columns)


def back_kernel(scale, mask_ref, key_ref, q_ref, g_ref, _, term_ref, grad_ref, stats_ref):
    block = key_ref.shape[1]
    mask = mask_ref[2 * block : 3 * block, :]
    keys = key_ref[...].T
    score = scores_of(scale, keys, mask, lanes(q_ref))
    grad_weight = dot(keys[:, : g_ref.shape[1]], g_ref[...], NT)
    grad_ref[...] = grad_weight
    partial_softmax(score, grad_weight, term_ref, stats_ref, slice(None))


def store_weights(terms, grad_weight, factor, delta, weight_ref, score_ref, span):
    weight = terms * factor
    grad_score = (weight * (grad_weight - delta)).astype(BF16)
    weight = weight.astype(BF16)
    size = weight_ref.shape[2]
    for n in range(weight_ref.shape[0]):
        weight_ref[n, span, :] = weight[:, n * size : (n + 1) * size]
        score_ref[n, span, :] = grad_score[:, n * size : (n + 1) * size]
    return weight, grad_score


def key_grads(scale, q_cols, g_rows, weight, grad_score, grad_ref):
    grad_ref[...] = dot(q_cols, grad_score, NT) * scale
    grad_ref[: g_rows.shape[1], :] += dot(weight, g_rows).T


def weights_kernel(scale, mask_ref, *refs):
    swap_ref, cross_ref, q_ref, g_ref, *known = refs[:6]
    weight_ref, score_ref, factors_ref, out_ref, grad_ref = refs[6:]
    keys = jnp.concatenate([swap_ref[...].T, cross_ref[...].T], axis=0)
    mask = mask_ref[: keys.shape[0], :]
    q_cols = lanes(q_ref)
    score = scores_of(scale, keys, mask, q_cols)
    grad_weight = dot(keys[:, : g_ref.shape[1]], g_ref[...], NT)
    top = jnp.max(score, axis=0, keepdims=True)
    for stats_ref in known:
        top = jnp.maximum(top, stats_ref[0:1, :])
    terms = jnp.exp2(score - top)
    total = jnp.sum(terms, axis=0, keepdims=True)
    delta = jnp.sum(terms * grad_weight, axis=0, keepdims=True)
    factors = []
    for stats_ref in known:
        factors.append(jnp.exp2(stats_ref[0:1, :] - top))
        total = total + factors[-1] * stats_ref[1:2, :]
        delta = delta + factors[-1] * stats_ref[2:3, :]
    inverse = 1.0 / total
    delta = delta * inverse
    factors_ref[0:1, :] = delta
    for n, factor in enumerate(factors):
        factors_ref[n + 1 : n + 2, :] = factor * inverse
    weight, grad_score = store_weights(
        terms, grad_weight, inverse, delta, weight_ref, score_ref, slice(None)
    )
    key_grads(scale, q_cols, g_ref[...], weight, grad_score, grad_ref)
    out_ref[...] = grad_ref[...].astype(BF16)


def keys_kernel(scale, q_ref, g_ref, factors_ref, *refs):
    *known, weight_ref, score_ref, grad_ref = refs
    delta = factors_ref[0:1, :]
    weights, grad_scores = [], []
    first = 0
    for n in range(len(known) // 2):
        term_ref, block_grad_ref = known[2 * n : 2 * n + 2]
        last = first + term_ref.shape[0]
        weight, grad_score = store_weights(
            term_ref[...],
            block_grad_ref[...],
            factors_ref[n + 1 : n + 2, :],
            delta,
            weight_ref,
            score_ref,
            slice(first, last),
        )
        weights.append(weight)
        grad_scores.append(grad_score)
        first = last
    weight = jnp.concatenate(weights, axis=0)
    grad_score = jnp.concatenate(grad_scores, axis=0)
    key_grads(scale, lanes(q_ref), g_ref[...], weight, grad_score, grad_ref)


def split_kernel(kept_ref, swap_ref, *refs):
    piece_refs = refs[:-1]
    total_ref = refs[-1]
    parts = len(piece_refs)
    block = kept_ref.shape[1] // 2
    odd = lax.rem(lax.axis_index("ctx"), 2) == 1
    crossed = swap_ref[:, block:].astype(F32)
    total_ref[:, :block] = jnp.where(odd, crossed, 0.0)
    total_ref[:, block : 2 * block] = kept_ref[:, :block] + swap_ref[:, :block].astype(F32)
    total_ref[:, 2 * block :] = kept_ref[:, block:] + jnp.where(odd, 0.0, crossed)
    share = total_ref.shape[0] // parts
    for n, piece_ref in enumerate(piece_refs):
        first = pl.multiple_of(lax.rem(lax.axis_index("head") + n, parts) * share, share)
        piece_ref[...] = total_ref[pl.ds(first, share), :].astype(piece_ref.dtype)


def regroup(few, heads):
    row = lax.broadcasted_iota(jnp.int32, (few * heads, few * heads), 0)
    col = lax.broadcasted_iota(jnp.int32, (few * heads, few * heads), 1)
    order = (row // few == col % heads) & (row % few == col // heads)
    return order.astype(F32).astype(BF16)


def forward_kernel(scale, *refs):
    key_refs = refs[:SLOTS]
    weight_refs = refs[SLOTS : SLOTS + 2]
    score_refs = refs[SLOTS + 2 : SLOTS + 4]
    att_to, gq_to, cols_ref, rows_ref, by_head_ref, att_ref, gq_ref, sems = refs[SLOTS + 4 :]
    joined = lambda parts, step: jnp.concatenate([part[step] for part in parts], axis=0)
    block = key_refs[0].shape[1]
    tokens, heads, latent_width = att_ref.shape
    steps = heads // PART
    copies = []

    def send(source, target, first, count):
        span = pl.ds(first, count)
        copies.append(
            pltpu.make_async_copy(source.at[span], target.at[span], sems.at[len(copies)])
        )
        copies[-1].start()

    def grad_queries(step):
        grad = dot(cols_ref[...], joined(score_refs, step)) * scale
        for n in range(PART):
            gq_ref[step * PART + n] = grad[:, n * block : (n + 1) * block]
        send(gq_ref, gq_to, step * PART, PART)

    for slot, key_ref in enumerate(key_refs):
        cols_ref[:, slot * block : (slot + 1) * block] = key_ref[...]
        rows_ref[slot * block : (slot + 1) * block, :] = key_ref[:latent_width, :].T
    grad_queries(0)
    span = PART * block
    for step in range(steps):
        att = dot(joined(weight_refs, step).T, rows_ref[...])
        by_head_ref[step * span : (step + 1) * span, :] = att.astype(BF16)
    few = 256 // heads
    order = regroup(few, heads)
    size = tokens // steps
    for chunk in range(steps):
        for first in range(chunk * size, (chunk + 1) * size, few):
            part = jnp.concatenate(
                [by_head_ref[h * tokens + first : h * tokens + first + few, :] for h in range(heads)],
                axis=0,
            )
            part = lax.dot_general(
                order, part, (((0,), (0,)), ((), ())), preferred_element_type=F32
            )
            att_ref[first : first + few] = part.astype(BF16).reshape(few, heads, latent_width)
        send(att_ref, att_to, chunk * size, size)
    for step in range(1, steps):
        grad_queries(step)
    for copy in copies:
        copy.wait()


def merge_kernel(own_ref, *refs):
    far_ref, back_ref, rest_ref = refs[-3:]
    total = own_ref[...]
    for ref in refs[:-4]:
        total = total + ref[...].astype(F32)
    block = rest_ref.shape[1]
    far_ref[...] = total[:, :block].astype(BF16)
    back_ref[...] = total[:, block : 2 * block].astype(BF16)
    rest_ref[...] = total[:, 2 * block :]


def add_kernel(*refs):
    total = refs[0][...]
    for ref in refs[1:-1]:
        total = total + ref[...].astype(F32)
    refs[-1][...] = total.astype(refs[-1].dtype)


def shards(queries, latent, grad_out, doc_start, block_list):
    block, heads, width = queries.shape
    latent_width = grad_out.shape[2]
    scale = 1.0 / math.sqrt(latent_width // 4 + width - latent_width)
    parts = lax.axis_size("head")
    share = width // parts
    keys = SLOTS * block
    steps = heads // PART
    rows = PART * block
    vmem = pl.BlockSpec(memory_space=pltpu.VMEM)
    smem = pl.BlockSpec(memory_space=pltpu.SMEM)
    anywhere = pl.BlockSpec(memory_space=pl.ANY)
    keep = lambda x: pltpu.with_memory_space_constraint(x, pltpu.VMEM)
    limit = lambda n: pltpu.CompilerParams(vmem_limit_bytes=n * MIB)

    latent_t = latent.T
    back = moved(latent_t, "ctx", lambda s: s + 2)
    crossed = moved(latent_t, "ctx", lambda s: s + 3 if s % 2 else s + 1)

    block_cost = pl.CostEstimate(
        flops=2 * heads * block * block * (width + latent_width),
        bytes_accessed=4 * MIB,
        transcendentals=0,
    )
    block_shapes = [pltpu.VMEM((n, heads * block), F32) for n in (block, block, 8)]
    in_hbm = lambda x: pltpu.with_memory_space_constraint(x, pltpu.HBM)
    own_terms, own_grad, own_stats, q_t, g_rows, mask, own_t, token = pl.pallas_call(
        functools.partial(own_kernel, scale),
        in_specs=[anywhere] * 5,
        out_specs=[vmem] * 8,
        out_shape=block_shapes
        + [
            pltpu.VMEM((heads, width, block), BF16),
            pltpu.VMEM((heads * block, latent_width), BF16),
            pltpu.VMEM((keys, block), F32),
            pltpu.VMEM((width, block), BF16),
            jax.ShapeDtypeStruct((8, 128), F32),
        ],
        scratch_shapes=[
            pltpu.SMEM(block_list.shape, jnp.int32),
            pltpu.VMEM((1, block), jnp.int32),
            pltpu.VMEM((block, heads, latent_width), BF16),
            pltpu.SemaphoreType.DMA((3 + sum(COPIES),)),
        ],
        compiler_params=limit(16),
        cost_estimate=block_cost,
        name="own",
    )(
        in_hbm(latent_t),
        in_hbm(block_list),
        in_hbm(doc_start.reshape(1, block)),
        in_hbm(grad_out),
        in_hbm(queries.transpose(1, 2, 0)),
    )
    g_rows, mask, own_t = keep(g_rows), keep(mask), keep(own_t)
    own_parts = [keep(x) for x in (own_terms, own_grad, own_stats)]
    q_t = keep(q_t)
    back, token = lax.optimization_barrier((back, token))
    swapped = moved(back, "ctx", lambda s: s ^ 1)
    back_parts = pl.pallas_call(
        functools.partial(back_kernel, scale),
        in_specs=[vmem] * 4 + [anywhere],
        out_specs=[vmem] * 3,
        out_shape=block_shapes,
        compiler_params=limit(16),
        cost_estimate=block_cost,
        name="back",
    )(mask, keep(back), q_t, g_rows, token)
    back_parts = [keep(x) for x in back_parts]
    window = [keep(swapped), keep(crossed), keep(back), own_t]

    half_shapes = [pltpu.VMEM((steps, keys // 2, rows), BF16)] * 2
    new_weight, new_score, factors, to_swap = pl.pallas_call(
        functools.partial(weights_kernel, scale),
        in_specs=[vmem] * 7,
        out_specs=[vmem] * 4,
        out_shape=half_shapes
        + [pltpu.VMEM((8, heads * block), F32), pltpu.VMEM((width, keys // 2), BF16)],
        scratch_shapes=[pltpu.VMEM((width, keys // 2), F32)],
        compiler_params=limit(28),
        cost_estimate=pl.CostEstimate(
            flops=2 * heads * block * keys * (width + latent_width),
            bytes_accessed=12 * MIB,
            transcendentals=heads * block * keys,
        ),
        name="weights",
    )(mask, *window[:2], q_t, g_rows, back_parts[2], own_parts[2])
    new_weight, new_score = keep(new_weight), keep(new_score)
    from_swap = moved(to_swap, "ctx", lambda s: s ^ 1)

    kept_weight, kept_score, kept = pl.pallas_call(
        functools.partial(keys_kernel, scale),
        in_specs=[vmem] * 7,
        out_specs=[vmem] * 3,
        out_shape=half_shapes + [pltpu.VMEM((width, keys // 2), F32)],
        compiler_params=limit(24),
        cost_estimate=pl.CostEstimate(
            flops=heads * block * keys * (width + latent_width),
            bytes_accessed=8 * MIB,
            transcendentals=0,
        ),
        name="keys",
    )(q_t, g_rows, keep(factors), *back_parts[:2], *own_parts[:2])
    kept_weight, kept_score = keep(kept_weight), keep(kept_score)

    own, *pieces = pl.pallas_call(
        split_kernel,
        in_specs=[vmem] * 2,
        out_specs=[vmem] * parts,
        out_shape=[
            pltpu.VMEM((share, 3 * block), BF16 if n else F32) for n in range(parts)
        ],
        scratch_shapes=[pltpu.VMEM((width, 3 * block), F32)],
        compiler_params=limit(4),
        name="split",
    )(keep(kept), keep(from_swap))
    arrived = [moved(piece, "head", lambda s, n=n: s + n + 1) for n, piece in enumerate(pieces)]

    att, gq = pl.pallas_call(
        functools.partial(forward_kernel, scale),
        in_specs=[vmem] * (SLOTS + 4),
        out_specs=[anywhere] * 2,
        out_shape=[
            pltpu.HBM((block, heads, latent_width), BF16),
            pltpu.HBM((heads, width, block), F32),
        ],
        scratch_shapes=[
            pltpu.VMEM((width, keys), BF16),
            pltpu.VMEM((keys, latent_width), BF16),
            pltpu.VMEM((heads * block, latent_width), BF16),
            pltpu.VMEM((block, heads, latent_width), BF16),
            pltpu.VMEM((heads, width, block), F32),
            pltpu.SemaphoreType.DMA((2 * steps,)),
        ],
        compiler_params=limit(28),
        cost_estimate=pl.CostEstimate(
            flops=2 * heads * block * keys * (width + latent_width),
            bytes_accessed=12 * MIB,
            transcendentals=0,
        ),
        name="forward",
    )(*window, new_weight, kept_weight, new_score, kept_score)

    to_far, to_back, rest = pl.pallas_call(
        merge_kernel,
        in_specs=[vmem] * parts + [anywhere],
        out_specs=[vmem] * 3,
        out_shape=[pltpu.VMEM((share, block), t) for t in (BF16, BF16, F32)],
        compiler_params=limit(4),
        name="merge",
    )(keep(own), *map(keep, arrived), in_hbm(att))
    from_back = moved(to_back, "ctx", lambda s: s - 2)
    from_far = moved(to_far, "ctx", lambda s: s - 4 if s % 2 else s - 2)
    total = pl.pallas_call(
        add_kernel,
        in_specs=[vmem] * 3,
        out_specs=vmem,
        out_shape=jax.ShapeDtypeStruct((share, block), F32),
        compiler_params=limit(1),
        name="total",
    )(*map(keep, (rest, from_back, from_far)))
    return (att, gq.transpose(2, 0, 1), total.T)


def solution(mesh):
    placed = (
        P("ctx", "head", None),
        P("ctx", None),
        P("ctx", "head", None),
        P("ctx"),
        P("ctx", None),
    )
    return jax.shard_map(
        shards,
        mesh=mesh,
        in_specs=placed,
        out_specs=(P("ctx", "head", None), P("ctx", "head", None), P("ctx", "head")),
        check_vma=False,
    )
```

```python
import functools
import math

import jax
import jax.numpy as jnp
from jax import lax
from jax.experimental import pallas as pl
from jax.experimental.pallas import tpu as pltpu
from jax.sharding import PartitionSpec as P

F32 = jnp.float32
BF16 = jnp.bfloat16
SLOTS = 4
PART = 4
COPIES = (2, 1)
MIB = 1 << 20
NN = (((1,), (0,)), ((), ()))
NT = (((1,), (1,)), ((), ()))


def moved(value, axis, target):
    count = lax.axis_size(axis)
    return lax.ppermute(value, axis, [(s, target(s) % count) for s in range(count)])


def dot(a, b, dims=NN):
    return lax.dot_general(a, b, dims, preferred_element_type=F32)


def lanes(ref):
    return jnp.concatenate([ref[n] for n in range(ref.shape[0])], axis=1)


def write_mask(mask_ref, entries_ref, start_ref):
    place = lax.axis_index("ctx")
    parity = lax.rem(place, 2)
    block = start_ref.shape[1]
    q_pos = place * block + lax.broadcasted_iota(jnp.int32, (block, block), 1)
    for slot, offset in enumerate((1 + 2 * parity, 3 - 2 * parity, 2, 0)):
        entry = place - offset
        listed = entries_ref[0, 0] == entry
        for n in range(1, entries_ref.shape[1]):
            listed = listed | (entries_ref[0, n] == entry)
        first = jnp.where(listed & (entry >= 0), entry * block, 1 << 24)
        k_pos = first + lax.broadcasted_iota(jnp.int32, (block, block), 0)
        allowed = (k_pos <= q_pos) & (k_pos >= start_ref[...])
        mask_ref[slot * block : (slot + 1) * block, :] = jnp.where(allowed, 0.0, -1e30)


def scores_of(scale, keys, mask, q_cols):
    heads = q_cols.shape[1] // mask.shape[1]
    mask = jnp.concatenate([mask] * heads, axis=1)
    return dot(keys, q_cols) * (scale * math.log2(math.e)) + mask


def partial_softmax(score, grad_weight, term_ref, stats_ref, span):
    top = jnp.max(score, axis=0, keepdims=True)
    terms = jnp.exp2(score - top)
    term_ref[:, span] = terms
    stats_ref[0:1, span] = top
    stats_ref[1:2, span] = jnp.sum(terms, axis=0, keepdims=True)
    stats_ref[2:3, span] = jnp.sum(terms * grad_weight, axis=0, keepdims=True)


def own_kernel(scale, key_from, entries_from, start_from, g_from, q_from, *refs):
    term_ref, grad_ref, stats_ref, q_ref, g_ref, mask_ref, key_ref, token_ref = refs[:8]
    entries_ref, start_ref, buffer_ref, sems = refs[8:]
    tokens, heads, latent_width = g_from.shape
    g_chunks, q_chunks = COPIES
    tables = [
        pltpu.make_async_copy(entries_from, entries_ref, sems.at[0]),
        pltpu.make_async_copy(start_from, start_ref, sems.at[1]),
        pltpu.make_async_copy(key_from, key_ref, sems.at[2]),
    ]
    size = tokens // g_chunks
    g_copies = [
        pltpu.make_async_copy(
            g_from.at[pl.ds(n * size, size)], buffer_ref.at[pl.ds(n * size, size)], sems.at[3 + n]
        )
        for n in range(g_chunks)
    ]
    part_heads = heads // q_chunks
    q_copies = [
        pltpu.make_async_copy(
            q_from.at[pl.ds(n * part_heads, part_heads)],
            q_ref.at[pl.ds(n * part_heads, part_heads)],
            sems.at[3 + g_chunks + n],
        )
        for n in range(q_chunks)
    ]
    for copy in tables + g_copies + q_copies:
        copy.start()
    token_ref[...] = jnp.zeros_like(token_ref)
    for copy in tables:
        copy.wait()
    keys = key_ref[...].T
    write_mask(mask_ref, entries_ref, start_ref)
    mask = mask_ref[mask_ref.shape[0] - keys.shape[0] :, :]

    few = 256 // heads
    order = regroup(few, heads)
    for n, copy in enumerate(g_copies):
        copy.wait()
        for first in range(n * size, (n + 1) * size, few):
            part = buffer_ref[first : first + few].reshape(few * heads, latent_width)
            part = dot(order, part).astype(BF16)
            for h in range(heads):
                g_ref[h * tokens + first : h * tokens + first + few, :] = part[
                    h * few : (h + 1) * few
                ]
    grad_ref[...] = dot(keys[:, :latent_width], g_ref[...], NT)
    span = part_heads * tokens
    for n, copy in enumerate(q_copies):
        copy.wait()
        q_cols = lanes(q_ref[n * part_heads : (n + 1) * part_heads])
        columns = slice(n * span, (n + 1) * span)
        score = scores_of(scale, keys, mask, q_cols)
        partial_softmax(score, grad_ref[:, columns], term_ref, stats_ref, columns)


def back_kernel(scale, mask_ref, key_ref, q_ref, g_ref, _, term_ref, grad_ref, stats_ref):
    block = key_ref.shape[1]
    mask = mask_ref[2 * block : 3 * block, :]
    keys = key_ref[...].T
    score = scores_of(scale, keys, mask, lanes(q_ref))
    grad_weight = dot(keys[:, : g_ref.shape[1]], g_ref[...], NT)
    grad_ref[...] = grad_weight
    partial_softmax(score, grad_weight, term_ref, stats_ref, slice(None))


def store_weights(terms, grad_weight, factor, delta, weight_ref, score_ref, span):
    weight = terms * factor
    grad_score = (weight * (grad_weight - delta)).astype(BF16)
    weight = weight.astype(BF16)
    size = weight_ref.shape[2]
    for n in range(weight_ref.shape[0]):
        weight_ref[n, span, :] = weight[:, n * size : (n + 1) * size]
        score_ref[n, span, :] = grad_score[:, n * size : (n + 1) * size]
    return weight, grad_score


def key_grads(scale, q_cols, g_rows, weight, grad_score, grad_ref):
    grad_ref[...] = dot(q_cols, grad_score, NT) * scale
    grad_ref[: g_rows.shape[1], :] += dot(weight, g_rows).T


def weights_kernel(scale, mask_ref, *refs):
    swap_ref, cross_ref, q_ref, g_ref, *known = refs[:6]
    weight_ref, score_ref, factors_ref, out_ref, grad_ref = refs[6:]
    keys = jnp.concatenate([swap_ref[...].T, cross_ref[...].T], axis=0)
    mask = mask_ref[: keys.shape[0], :]
    q_cols = lanes(q_ref)
    score = scores_of(scale, keys, mask, q_cols)
    grad_weight = dot(keys[:, : g_ref.shape[1]], g_ref[...], NT)
    top = jnp.max(score, axis=0, keepdims=True)
    for stats_ref in known:
        top = jnp.maximum(top, stats_ref[0:1, :])
    terms = jnp.exp2(score - top)
    total = jnp.sum(terms, axis=0, keepdims=True)
    delta = jnp.sum(terms * grad_weight, axis=0, keepdims=True)
    factors = []
    for stats_ref in known:
        factors.append(jnp.exp2(stats_ref[0:1, :] - top))
        total = total + factors[-1] * stats_ref[1:2, :]
        delta = delta + factors[-1] * stats_ref[2:3, :]
    inverse = 1.0 / total
    delta = delta * inverse
    factors_ref[0:1, :] = delta
    for n, factor in enumerate(factors):
        factors_ref[n + 1 : n + 2, :] = factor * inverse
    weight, grad_score = store_weights(
        terms, grad_weight, inverse, delta, weight_ref, score_ref, slice(None)
    )
    key_grads(scale, q_cols, g_ref[...], weight, grad_score, grad_ref)
    out_ref[...] = grad_ref[...].astype(BF16)


def keys_kernel(scale, q_ref, g_ref, factors_ref, *refs):
    *known, weight_ref, score_ref, grad_ref = refs
    delta = factors_ref[0:1, :]
    weights, grad_scores = [], []
    first = 0
    for n in range(len(known) // 2):
        term_ref, block_grad_ref = known[2 * n : 2 * n + 2]
        last = first + term_ref.shape[0]
        weight, grad_score = store_weights(
            term_ref[...],
            block_grad_ref[...],
            factors_ref[n + 1 : n + 2, :],
            delta,
            weight_ref,
            score_ref,
            slice(first, last),
        )
        weights.append(weight)
        grad_scores.append(grad_score)
        first = last
    weight = jnp.concatenate(weights, axis=0)
    grad_score = jnp.concatenate(grad_scores, axis=0)
    key_grads(scale, lanes(q_ref), g_ref[...], weight, grad_score, grad_ref)


def split_kernel(kept_ref, swap_ref, *refs):
    piece_refs = refs[:-1]
    total_ref = refs[-1]
    parts = len(piece_refs)
    block = kept_ref.shape[1] // 2
    odd = lax.rem(lax.axis_index("ctx"), 2) == 1
    crossed = swap_ref[:, block:].astype(F32)
    total_ref[:, :block] = jnp.where(odd, crossed, 0.0)
    total_ref[:, block : 2 * block] = kept_ref[:, :block] + swap_ref[:, :block].astype(F32)
    total_ref[:, 2 * block :] = kept_ref[:, block:] + jnp.where(odd, 0.0, crossed)
    share = total_ref.shape[0] // parts
    for n, piece_ref in enumerate(piece_refs):
        first = pl.multiple_of(lax.rem(lax.axis_index("head") + n, parts) * share, share)
        piece_ref[...] = total_ref[pl.ds(first, share), :].astype(piece_ref.dtype)


def regroup(few, heads):
    row = lax.broadcasted_iota(jnp.int32, (few * heads, few * heads), 0)
    col = lax.broadcasted_iota(jnp.int32, (few * heads, few * heads), 1)
    order = (row // few == col % heads) & (row % few == col // heads)
    return order.astype(F32).astype(BF16)


def forward_kernel(scale, *refs):
    key_refs = refs[:SLOTS]
    weight_refs = refs[SLOTS : SLOTS + 2]
    score_refs = refs[SLOTS + 2 : SLOTS + 4]
    att_to, gq_to, cols_ref, rows_ref, by_head_ref, att_ref, gq_ref, sems = refs[SLOTS + 4 :]
    joined = lambda parts, step: jnp.concatenate([part[step] for part in parts], axis=0)
    block = key_refs[0].shape[1]
    tokens, heads, latent_width = att_ref.shape
    steps = heads // PART
    copies = []

    def send(source, target, first, count):
        span = pl.ds(first, count)
        copies.append(
            pltpu.make_async_copy(source.at[span], target.at[span], sems.at[len(copies)])
        )
        copies[-1].start()

    def grad_queries(step):
        grad = dot(cols_ref[...], joined(score_refs, step)) * scale
        for n in range(PART):
            gq_ref[step * PART + n] = grad[:, n * block : (n + 1) * block]
        send(gq_ref, gq_to, step * PART, PART)

    for slot, key_ref in enumerate(key_refs):
        cols_ref[:, slot * block : (slot + 1) * block] = key_ref[...]
        rows_ref[slot * block : (slot + 1) * block, :] = key_ref[:latent_width, :].T
    grad_queries(0)
    span = PART * block
    for step in range(steps):
        att = dot(joined(weight_refs, step).T, rows_ref[...])
        by_head_ref[step * span : (step + 1) * span, :] = att.astype(BF16)
    few = 256 // heads
    order = regroup(few, heads)
    size = tokens // steps
    for chunk in range(steps):
        for first in range(chunk * size, (chunk + 1) * size, few):
            part = jnp.concatenate(
                [by_head_ref[h * tokens + first : h * tokens + first + few, :] for h in range(heads)],
                axis=0,
            )
            part = lax.dot_general(
                order, part, (((0,), (0,)), ((), ())), preferred_element_type=F32
            )
            att_ref[first : first + few] = part.astype(BF16).reshape(few, heads, latent_width)
        send(att_ref, att_to, chunk * size, size)
    for step in range(1, steps):
        grad_queries(step)
    for copy in copies:
        copy.wait()


def merge_kernel(own_ref, *refs):
    far_ref, back_ref, rest_ref = refs[-3:]
    total = own_ref[...]
    for ref in refs[:-4]:
        total = total + ref[...].astype(F32)
    block = rest_ref.shape[1]
    far_ref[...] = total[:, :block].astype(BF16)
    back_ref[...] = total[:, block : 2 * block].astype(BF16)
    rest_ref[...] = total[:, 2 * block :]


def add_kernel(*refs):
    total = refs[0][...]
    for ref in refs[1:-1]:
        total = total + ref[...].astype(F32)
    refs[-1][...] = total.astype(refs[-1].dtype)


def shards(queries, latent, grad_out, doc_start, block_list):
    block, heads, width = queries.shape
    latent_width = grad_out.shape[2]
    scale = 1.0 / math.sqrt(latent_width // 4 + width - latent_width)
    parts = lax.axis_size("head")
    share = width // parts
    keys = SLOTS * block
    steps = heads // PART
    rows = PART * block
    vmem = pl.BlockSpec(memory_space=pltpu.VMEM)
    smem = pl.BlockSpec(memory_space=pltpu.SMEM)
    anywhere = pl.BlockSpec(memory_space=pl.ANY)
    keep = lambda x: pltpu.with_memory_space_constraint(x, pltpu.VMEM)
    limit = lambda n: pltpu.CompilerParams(vmem_limit_bytes=n * MIB)

    latent_t = latent.T
    back = moved(latent_t, "ctx", lambda s: s + 2)
    crossed = moved(latent_t, "ctx", lambda s: s + 3 if s % 2 else s + 1)

    block_cost = pl.CostEstimate(
        flops=2 * heads * block * block * (width + latent_width),
        bytes_accessed=4 * MIB,
        transcendentals=0,
    )
    block_shapes = [pltpu.VMEM((n, heads * block), F32) for n in (block, block, 8)]
    in_hbm = lambda x: pltpu.with_memory_space_constraint(x, pltpu.HBM)
    own_terms, own_grad, own_stats, q_t, g_rows, mask, own_t, token = pl.pallas_call(
        functools.partial(own_kernel, scale),
        in_specs=[anywhere] * 5,
        out_specs=[vmem] * 8,
        out_shape=block_shapes
        + [
            pltpu.VMEM((heads, width, block), BF16),
            pltpu.VMEM((heads * block, latent_width), BF16),
            pltpu.VMEM((keys, block), F32),
            pltpu.VMEM((width, block), BF16),
            jax.ShapeDtypeStruct((8, 128), F32),
        ],
        scratch_shapes=[
            pltpu.SMEM(block_list.shape, jnp.int32),
            pltpu.VMEM((1, block), jnp.int32),
            pltpu.VMEM((block, heads, latent_width), BF16),
            pltpu.SemaphoreType.DMA((3 + sum(COPIES),)),
        ],
        compiler_params=limit(16),
        cost_estimate=block_cost,
        name="own",
    )(
        in_hbm(latent_t),
        in_hbm(block_list),
        in_hbm(doc_start.reshape(1, block)),
        in_hbm(grad_out),
        in_hbm(queries.transpose(1, 2, 0)),
    )
    g_rows, mask, own_t = keep(g_rows), keep(mask), keep(own_t)
    own_parts = [keep(x) for x in (own_terms, own_grad, own_stats)]
    q_t = keep(q_t)
    back, token = lax.optimization_barrier((back, token))
    swapped = moved(back, "ctx", lambda s: s ^ 1)
    back_parts = pl.pallas_call(
        functools.partial(back_kernel, scale),
        in_specs=[vmem] * 4 + [anywhere],
        out_specs=[vmem] * 3,
        out_shape=block_shapes,
        compiler_params=limit(16),
        cost_estimate=block_cost,
        name="back",
    )(mask, keep(back), q_t, g_rows, token)
    back_parts = [keep(x) for x in back_parts]
    window = [keep(swapped), keep(crossed), keep(back), own_t]

    half_shapes = [pltpu.VMEM((steps, keys // 2, rows), BF16)] * 2
    new_weight, new_score, factors, to_swap = pl.pallas_call(
        functools.partial(weights_kernel, scale),
        in_specs=[vmem] * 7,
        out_specs=[vmem] * 4,
        out_shape=half_shapes
        + [pltpu.VMEM((8, heads * block), F32), pltpu.VMEM((width, keys // 2), BF16)],
        scratch_shapes=[pltpu.VMEM((width, keys // 2), F32)],
        compiler_params=limit(28),
        cost_estimate=pl.CostEstimate(
            flops=2 * heads * block * keys * (width + latent_width),
            bytes_accessed=12 * MIB,
            transcendentals=heads * block * keys,
        ),
        name="weights",
    )(mask, *window[:2], q_t, g_rows, back_parts[2], own_parts[2])
    new_weight, new_score = keep(new_weight), keep(new_score)
    from_swap = moved(to_swap, "ctx", lambda s: s ^ 1)

    kept_weight, kept_score, kept = pl.pallas_call(
        functools.partial(keys_kernel, scale),
        in_specs=[vmem] * 7,
        out_specs=[vmem] * 3,
        out_shape=half_shapes + [pltpu.VMEM((width, keys // 2), F32)],
        compiler_params=limit(24),
        cost_estimate=pl.CostEstimate(
            flops=heads * block * keys * (width + latent_width),
            bytes_accessed=8 * MIB,
            transcendentals=0,
        ),
        name="keys",
    )(q_t, g_rows, keep(factors), *back_parts[:2], *own_parts[:2])
    kept_weight, kept_score = keep(kept_weight), keep(kept_score)

    own, *pieces = pl.pallas_call(
        split_kernel,
        in_specs=[vmem] * 2,
        out_specs=[vmem] * parts,
        out_shape=[
            pltpu.VMEM((share, 3 * block), BF16 if n else F32) for n in range(parts)
        ],
        scratch_shapes=[pltpu.VMEM((width, 3 * block), F32)],
        compiler_params=limit(4),
        name="split",
    )(keep(kept), keep(from_swap))
    arrived = [moved(piece, "head", lambda s, n=n: s + n + 1) for n, piece in enumerate(pieces)]

    att, gq = pl.pallas_call(
        functools.partial(forward_kernel, scale),
        in_specs=[vmem] * (SLOTS + 4),
        out_specs=[anywhere] * 2,
        out_shape=[
            pltpu.HBM((block, heads, latent_width), BF16),
            pltpu.HBM((heads, width, block), F32),
        ],
        scratch_shapes=[
            pltpu.VMEM((width, keys), BF16),
            pltpu.VMEM((keys, latent_width), BF16),
            pltpu.VMEM((heads * block, latent_width), BF16),
            pltpu.VMEM((block, heads, latent_width), BF16),
            pltpu.VMEM((heads, width, block), F32),
            pltpu.SemaphoreType.DMA((2 * steps,)),
        ],
        compiler_params=limit(28),
        cost_estimate=pl.CostEstimate(
            flops=2 * heads * block * keys * (width + latent_width),
            bytes_accessed=12 * MIB,
            transcendentals=0,
        ),
        name="forward",
    )(*window, new_weight, kept_weight, new_score, kept_score)

    to_far, to_back, rest = pl.pallas_call(
        merge_kernel,
        in_specs=[vmem] * parts + [anywhere],
        out_specs=[vmem] * 3,
        out_shape=[pltpu.VMEM((share, block), t) for t in (BF16, BF16, F32)],
        compiler_params=limit(4),
        name="merge",
    )(keep(own), *map(keep, arrived), in_hbm(att))
    from_back = moved(to_back, "ctx", lambda s: s - 2)
    from_far = moved(to_far, "ctx", lambda s: s - 4 if s % 2 else s - 2)
    total = pl.pallas_call(
        add_kernel,
        in_specs=[vmem] * 3,
        out_specs=vmem,
        out_shape=jax.ShapeDtypeStruct((share, block), F32),
        compiler_params=limit(1),
        name="total",
    )(*map(keep, (rest, from_back, from_far)))
    return (att, gq.transpose(2, 0, 1), total.T)


def solution(mesh):
    placed = (
        P("ctx", "head", None),
        P("ctx", None),
        P("ctx", "head", None),
        P("ctx"),
        P("ctx", None),
    )
    return jax.shard_map(
        shards,
        mesh=mesh,
        in_specs=placed,
        out_specs=(P("ctx", "head", None), P("ctx", "head", None), P("ctx", "head")),
        check_vma=False,
    )
```
